256 devices in a mesh: gx: 16 (over x, y), gy: 16 (over z, core).
Axes of the slice: x: 4, y: 4, z: 8, core: 2. Of those that a mesh axis runs over, the one named last changes fastest.
Arguments:
- members: float32 [4, 2048, 2048], P(None, 'gy', 'gx'), may hold values from -6 to 6
- analysis: float32 [2048, 2048], P('gy', 'gx'), may hold values from -6 to 6
- land_sea: int32 [2048, 2048], P('gy', 'gx'), may hold values 0 or 1
Outputs:
- member_grad: float32 [4, 2048, 2048], P(None, 'gy', 'gx')
The draws below stay inside these ranges and needn't reach their ends.
All inputs are finite; a program needn't handle non-finite values. No bound on the sum of `land_sea` on one device may be relied on, other than what follows from the above.
Results may differ from the reference program's by a relative error of at most 0.00002.
Values sent between devices are 32-bit elements; how exact they have to be, the bound alone decides.
A program may use at most 64 MiB of HBM per device.

```python
import jax
import jax.numpy as jnp
from jax import lax

M = 4
H1 = 4
H2 = 16
H3 = 64
NY = 2048
NX = 2048


def with_ends(values, own_key, least, largest):
    extent = values.shape
    spot = [jax.random.randint(jax.random.fold_in(own_key, axis), (), 0, extent[axis]) for axis in range(len(extent))]
    values = values.at[tuple(spot)].set(least)
    longest = extent.index(max(extent))
    spot[longest] = (spot[longest] + 1) % extent[longest]
    return values.at[tuple(spot)].set(largest)


def block_scale(stream_key, dims, shards, least, high):
    def one(dim, parts):
        heights = jax.random.uniform(jax.random.fold_in(jax.random.fold_in(stream_key, 6), dim), (parts,), jnp.float32, least / len(shards), high / len(shards))
        return jnp.repeat(jnp.exp(heights), dims[dim] // parts).reshape((-1,) + (1,) * (len(dims) - dim - 1))

    factor_of = one(*shards[0])
    for cut in shards[1:]:
        factor_of = factor_of * one(*cut)
    return factor_of


def centred(key, dims, width, bound, split=(), held_as=jnp.bfloat16):
    factor_of = block_scale(key, dims, split, -0.22, 0.18) if split else 1.0
    values = jax.random.normal(key, dims, jnp.float32) * width * factor_of
    return jnp.minimum(jnp.maximum(values, -bound), bound).astype(held_as)


def setup_inputs(seed: int = 0) -> dict:
    seeds = jax.random.split(jax.random.key(seed), 4)
    members = centred(seeds[0], (M, NY, NX), 1.0, 6.0, ((1, 16), (2, 16)), jnp.float32)
    analysis = centred(seeds[1], (NY, NX), 1.0, 6.0, ((0, 16), (1, 16)), jnp.float32)
    land_sea = with_ends((jax.random.randint(seeds[2], (NY, NX), 0, 4) < 3).astype(jnp.int32), jax.random.fold_in(seeds[2], 1), 0, 1)
    return dict(members=members, analysis=analysis, land_sea=land_sea)


smooth_sq = 0.01

def box_sum(field, radius, along):
    length = field.shape[along] - 2 * radius
    running = jnp.cumsum(field, axis=along)
    leading = jnp.zeros_like(lax.slice_in_dim(running, 0, 1, axis=along))
    running = jnp.concatenate([leading, running], axis=along)
    upper = lax.slice_in_dim(running, 2 * radius + 1, 2 * radius + 1 + length, axis=along)
    lower = lax.slice_in_dim(running, 0, length, axis=along)
    return upper - lower

def pool(field, radius):
    return box_sum(box_sum(field, radius, 1), radius, 2) / (2 * radius + 1)

def slope_of(gap_value):
    return gap_value * lax.rsqrt(gap_value * gap_value + smooth_sq)

def score_slope(pooled, truth, weight):
    count = pooled.shape[0]
    own_slope = slope_of(pooled - truth[None])
    spread = jnp.zeros_like(pooled)
    for other in range(count):
        spread = spread + slope_of(pooled - pooled[other][None])
    return weight[None] * (own_slope / count - spread / (count * (count - 1)))

def reference(members, analysis, land_sea):
    weight = land_sea.astype(members.dtype)
    fields = jnp.concatenate([members, analysis[None]], axis=0)
    gradient_sum = jnp.zeros_like(members)
    for radius in (H1, H2, H3):
        padded = jnp.pad(fields, ((0, 0), (radius, radius), (radius, radius)))
        pooled = pool(padded, radius)
        slope_map = score_slope(pooled[:M], pooled[M], weight)
        gradient_sum = gradient_sum + pool(jnp.pad(slope_map, ((0, 0), (radius, radius), (radius, radius))), radius)
    return gradient_sum
```

```python
import jax
import jax.numpy as jnp
from jax import lax
from jax.experimental import pallas as pl
from jax.experimental.pallas import tpu as pltpu
from jax.sharding import PartitionSpec as P

RADII = (64, 16, 4)
PAD = 64
T = 128
E = T + 2 * PAD
MESH = pl.DeviceIdType.MESH
F32 = jnp.float32
BF16 = jnp.bfloat16


def split(value, terms):
    parts = []
    for _ in range(terms - 1):
        head = value.astype(BF16)
        parts.append(head)
        value = value - head.astype(F32)
    parts.append(value.astype(BF16))
    return parts


def dot(a, b):
    return jnp.dot(a, b, preferred_element_type=F32)


def side_column(lane, odd):
    if odd:
        return jnp.where(lane < PAD, lane - PAD, lane + PAD)
    return jnp.where(lane < PAD, lane + T, lane - T)


def band(a, b, radius):
    return jnp.where(jnp.abs(a - b) <= radius, 1.0, 0.0).astype(BF16)


def slope(gap, soft):
    return gap * lax.rsqrt(gap * gap + soft)


def kernel(
    mem_hbm, ana_hbm, land_hbm, out_ref,
    mem, ana, land, ctr, lft, rgt, go_l, go_r,
    vm, vt, hm, ht, sig,
    own2, s_r, s_l, q_r, q_l, ud, in_l, in_r, k_l, k_r,
    in_sem, ss, rs,
):
    gx, gy = lax.axis_index("gx"), lax.axis_index("gy")
    last_x, last_y = lax.axis_size("gx") - 1, lax.axis_size("gy") - 1
    par = lax.rem(gy, 2)
    mate = gy + 1 - 2 * par
    outer = gy - 1 + 2 * par
    has_l, has_r = gx > 0, gx < last_x
    has_o = jnp.logical_and(outer >= 0, outer <= last_y)
    has_ol, has_or = jnp.logical_and(has_l, has_o), jnp.logical_and(has_r, has_o)
    always = None

    def when(cond, fn):
        if cond is None:
            fn()
        else:
            pl.when(cond)(fn)

    dev = {
        "l": (gx - 1, gy), "r": (gx + 1, gy), "m": (gx, mate), "o": (gx, outer),
        "ol": (gx - 1, outer), "or": (gx + 1, outer),
    }
    to = {"l": has_l, "r": has_r, "m": always, "o": has_o, "ol": has_ol, "or": has_or}
    come = {"l": has_r, "r": has_l, "m": always, "o": has_o, "ol": has_or, "or": has_ol}

    barrier = pltpu.get_barrier_semaphore()
    for name in dev:
        def hello(name=name):
            pl.semaphore_signal(barrier, inc=1, device_id=dev[name], device_id_type=MESH)
        when(to[name], hello)

    loads = [
        pltpu.make_async_copy(mem_hbm, mem, in_sem.at[0]),
        pltpu.make_async_copy(ana_hbm, ana, in_sem.at[1]),
        pltpu.make_async_copy(land_hbm, land, in_sem.at[2]),
    ]
    for load in loads:
        load.start()

    def rows64(start):
        return pl.ds(pl.multiple_of(start, PAD), PAD)

    inner_src, inner_dst = rows64(2 * PAD - PAD * par), rows64(3 * PAD * par)
    outer_src, outer_dst = rows64(PAD + PAD * par), rows64(3 * PAD - 3 * PAD * par)
    to_mate, to_outer = rows64(3 * PAD - 3 * PAD * par), rows64(3 * PAD * par)
    near_mate, near_outer = rows64(PAD - PAD * par), rows64(PAD * par)
    mates_near, outers_near = rows64(PAD * par), rows64(PAD - PAD * par)
    body = pl.ds(PAD, T)
    lane = lax.broadcasted_iota(jnp.int32, (T, T), 1)
    low = lane < PAD
    low2 = lax.broadcasted_iota(jnp.int32, (E, T), 1) < PAD

    count = [0]
    sent = []

    def send(name, src, dst, only=None):
        k = count[0]
        count[0] += 1
        copy = pltpu.make_async_remote_copy(
            src_ref=src, dst_ref=dst, send_sem=ss.at[k], recv_sem=rs.at[k],
            device_id=dev[name], device_id_type=MESH,
        )
        here, there = (to[name], come[name]) if only is None else (only, only)
        when(here, copy.start)
        sent.append((here, copy))
        return there, copy

    def arrived(item):
        when(item[0], item[1].wait_recv)

    def fill(cond, ref, rows=None):
        def zero():
            if rows is None:
                ref[...] = jnp.zeros(ref.shape, ref.dtype)
            else:
                ref[:, rows, :] = jnp.zeros((ref.shape[0], PAD, T), ref.dtype)
        pl.when(cond)(zero)

    loads[0].wait()
    loads[1].wait()
    for m in range(4):
        ctr[m, body] = mem[m] - ana[...]
    for p in range(2):
        even = ctr[2 * p, body]
        odd = pltpu.roll(ctr[2 * p + 1, body], PAD, 1)
        go_r[p] = jnp.where(low, odd, even)
        go_l[p] = jnp.where(low, even, odd)

    peers = sum(c.astype(jnp.int32) for c in (has_l, has_r, has_o, has_ol, has_or)) + 1
    pl.semaphore_wait(barrier, peers)

    mains = []
    for p in range(2):
        mains.append(send("l", go_l.at[p], rgt.at[p, body]))
        mains.append(send("r", go_r.at[p], lft.at[p, body]))
    to_o = send("o", ctr.at[:, outer_src], ctr.at[:, outer_dst])
    to_m = send("m", ctr.at[:, inner_src], ctr.at[:, inner_dst])
    corners = [
        send("ol", go_l.at[:, near_outer], rgt.at[:, outer_dst]),
        send("or", go_r.at[:, near_outer], lft.at[:, outer_dst]),
    ]

    no_l, no_r, no_o = jnp.logical_not(has_l), jnp.logical_not(has_r), jnp.logical_not(has_o)
    edge = to_outer
    fill(no_l, lft)
    fill(no_r, rgt)
    fill(jnp.logical_and(no_o, has_l), lft, edge)
    fill(jnp.logical_and(no_o, has_r), rgt, edge)
    fill(no_o, ctr, edge)
    fill(no_l, in_l)
    fill(no_r, in_r)
    fill(no_o, ud, near_outer)
    fill(jnp.logical_not(has_ol), k_l, near_outer)
    fill(jnp.logical_not(has_or), k_r, near_outer)
    k_l[:, near_mate, :] = jnp.zeros((2, PAD, T), F32)
    k_r[:, near_mate, :] = jnp.zeros((2, PAD, T), F32)

    def iota(shape, axis):
        return lax.broadcasted_iota(jnp.int32, shape, axis)

    for i, r in enumerate(RADII):
        vm[pl.ds(i * T, T), :] = band(iota((T, E), 0), iota((T, E), 1) - PAD, r)
        vt[i] = band(iota((E, T), 0) - PAD, iota((E, T), 1), r)
        for odd in range(2):
            hm[odd, i, pl.ds(0, T)] = band(iota((T, T), 0), iota((T, T), 1), r)
            hm[odd, i, pl.ds(T, T)] = band(side_column(iota((T, T), 0), odd), iota((T, T), 1), r)
            ht[odd, pl.ds(i * T, T), pl.ds(0, T)] = band(iota((T, T), 0), iota((T, T), 1), r)
            ht[odd, pl.ds(i * T, T), pl.ds(T, T)] = band(iota((T, T), 0), side_column(iota((T, T), 1), odd), r)

    arrived(to_m)
    arrived(to_o)
    v_own = []
    for p in range(2):
        wide = jnp.concatenate([ctr[2 * p], ctr[2 * p + 1]], axis=1)
        v_own.append(sum(dot(vm[...], part) for part in split(wide, 3)))

    forwards = []
    for p in range(2):
        arrived(mains[2 * p])
        arrived(mains[2 * p + 1])
        forwards.append(send("m", lft.at[p, inner_src], lft.at[p, inner_dst], has_l))
        forwards.append(send("m", rgt.at[p, inner_src], rgt.at[p, inner_dst], has_r))
    for item in corners + forwards:
        arrived(item)

    pooled = [[None] * 4 for _ in RADII]
    for p in range(2):
        a, b = lft[p], rgt[p]
        wide = jnp.concatenate([jnp.where(low2, b, a), jnp.where(low2, a, b)], axis=1)
        v_side = sum(dot(vm[...], part) for part in split(wide, 3))
        for odd in range(2):
            for i in range(3):
                rows, cols = slice(i * T, (i + 1) * T), slice(odd * T, (odd + 1) * T)
                both = jnp.concatenate([v_own[p][rows, cols], v_side[rows, cols]], axis=1)
                pooled[i][2 * p + odd] = sum(dot(part, hm[odd, i]) for part in split(both, 3))

    loads[2].wait()
    weight = land[...].astype(F32)
    for i, r in enumerate(RADII):
        soft = 0.01 * (2 * r + 1) ** 2
        one, two = weight * (1 / (4 * (2 * r + 1))), weight * (1 / (12 * (2 * r + 1)))
        q = pooled[i]
        spread = [None] * 4
        for j in range(4):
            for k in range(j + 1, 4):
                s = slope(q[j] - q[k], soft)
                spread[j] = s if spread[j] is None else spread[j] + s
                spread[k] = -s if spread[k] is None else spread[k] - s
        for j in range(4):
            value = one * slope(q[j], soft) - two * spread[j]
            for h, part in enumerate(split(value, 2)):
                sig[h, i, :, pl.ds(j * T, T)] = part

    second = []
    for p in range(2):
        frame = []
        tall = [
            sum(dot(vt[i], sig[h, i, :, pl.ds(2 * p * T, 2 * T)]) for h in range(2)) for i in range(3)
        ]
        for odd in range(2):
            cols = slice(odd * T, (odd + 1) * T)
            flat = jnp.concatenate([t[:, cols] for t in tall], axis=1)
            full = sum(dot(part, ht[odd]) for part in split(flat, 2))
            own2[2 * p + odd] = full[:, :T]
            frame.append(full[:, T:])
        s_r[p] = jnp.where(low2, frame[0], frame[1])
        s_l[p] = jnp.where(low2, frame[1], frame[0])
        give = [
            send("m", s_r.at[p, to_mate], q_r.at[p]),
            send("m", s_l.at[p, to_mate], q_l.at[p]),
        ]
        second.append(send("l", s_l.at[p, outer_src], in_r.at[p, near_outer]))
        second.append(send("r", s_r.at[p, outer_src], in_l.at[p, near_outer]))
        second.append(send("ol", s_l.at[p, to_outer], k_r.at[p, outers_near]))
        second.append(send("or", s_r.at[p, to_outer], k_l.at[p, outers_near]))
        both = pl.ds(2 * p, 2)
        second.append(send("m", own2.at[both, to_mate], ud.at[both, mates_near]))
        second.append(send("o", own2.at[both, to_outer], ud.at[both, outers_near]))
        for item in give:
            arrived(item)
        s_r[p, inner_src] = s_r[p, inner_src] + q_r[p]
        s_l[p, inner_src] = s_l[p, inner_src] + q_l[p]
        second.append(send("l", s_l.at[p, inner_src], in_r.at[p, near_mate]))
        second.append(send("r", s_r.at[p, inner_src], in_l.at[p, near_mate]))

    for item in second:
        arrived(item)
    for p in range(2):
        a, b = in_l[p] + k_l[p], in_r[p] + k_r[p]
        e, o = 2 * p, 2 * p + 1
        out_ref[e] = own2[e, body] + ud[e] + jnp.where(low, a, b)
        out_ref[o] = own2[o, body] + ud[o] + pltpu.roll(jnp.where(low, b, a), PAD, 1)
    for here, copy in sent:
        when(here, copy.wait_send)


def local(members, analysis, land_sea):
    vmem = pltpu.VMEM
    return pl.pallas_call(
        kernel,
        out_shape=jax.ShapeDtypeStruct((4, T, T), F32),
        in_specs=[pl.BlockSpec(memory_space=pl.ANY)] * 3,
        out_specs=pl.BlockSpec(memory_space=vmem),
        scratch_shapes=[
            vmem((4, T, T), F32), vmem((T, T), F32), vmem((T, T), jnp.int32),
            vmem((4, E, T), F32), vmem((2, E, T), F32), vmem((2, E, T), F32),
            vmem((2, T, T), F32), vmem((2, T, T), F32),
            vmem((3 * T, E), BF16), vmem((3, E, T), BF16),
            vmem((2, 3, E, T), BF16), vmem((2, 3 * T, E), BF16),
            vmem((2, 3, T, 4 * T), BF16),
            vmem((4, E, T), F32), vmem((2, E, T), F32), vmem((2, E, T), F32),
            vmem((2, PAD, T), F32), vmem((2, PAD, T), F32),
            vmem((4, T, T), F32),
            vmem((2, T, T), F32), vmem((2, T, T), F32), vmem((2, T, T), F32), vmem((2, T, T), F32),
            pltpu.SemaphoreType.DMA((3,)),
            pltpu.SemaphoreType.DMA((32,)), pltpu.SemaphoreType.DMA((32,)),
        ],
        compiler_params=pltpu.CompilerParams(
            collective_id=0, has_side_effects=True, vmem_limit_bytes=40 * 1024 * 1024
        ),
    )(members, analysis, land_sea)


def solution(mesh):
    return jax.shard_map(
        local,
        mesh=mesh,
        in_specs=(P(None, "gy", "gx"), P("gy", "gx"), P("gy", "gx")),
        out_specs=P(None, "gy", "gx"),
        check_vma=False,
    )
```

```python
import jax
import jax.numpy as jnp
from jax import lax
from jax.experimental import pallas as pl
from jax.experimental.pallas import tpu as pltpu
from jax.sharding import PartitionSpec as P

RADII = (64, 16, 4)
PAD = 64
T = 128
E = T + 2 * PAD
MESH = pl.DeviceIdType.MESH
F32 = jnp.float32
BF16 = jnp.bfloat16


def split(value, terms):
    parts = []
    for _ in range(terms - 1):
        head = value.astype(BF16)
        parts.append(head)
        value = value - head.astype(F32)
    parts.append(value.astype(BF16))
    return parts


def dot(a, b):
    return jnp.dot(a, b, preferred_element_type=F32)


def side_column(lane, odd):
    if odd:
        return jnp.where(lane < PAD, lane - PAD, lane + PAD)
    return jnp.where(lane < PAD, lane + T, lane - T)


def band(a, b, radius):
    return jnp.where(jnp.abs(a - b) <= radius, 1.0, 0.0).astype(BF16)


def slope(gap, soft):
    return gap * lax.rsqrt(gap * gap + soft)


def kernel(
    mem_hbm, ana_hbm, land_hbm, out_ref,
    mem, ana, land, ctr, lft, rgt, go_l, go_r,
    vm, vt, hm, ht, sig,
    own2, s_r, s_l, q_r, q_l, ud, in_l, in_r, k_l, k_r,
    in_sem, ss, rs,
):
    gx, gy = lax.axis_index("gx"), lax.axis_index("gy")
    last_x, last_y = lax.axis_size("gx") - 1, lax.axis_size("gy") - 1
    par = lax.rem(gy, 2)
    mate = gy + 1 - 2 * par
    outer = gy - 1 + 2 * par
    has_l, has_r = gx > 0, gx < last_x
    has_o = jnp.logical_and(outer >= 0, outer <= last_y)
    has_ol, has_or = jnp.logical_and(has_l, has_o), jnp.logical_and(has_r, has_o)
    always = None

    def when(cond, fn):
        if cond is None:
            fn()
        else:
            pl.when(cond)(fn)

    dev = {
        "l": (gx - 1, gy), "r": (gx + 1, gy), "m": (gx, mate), "o": (gx, outer),
        "ol": (gx - 1, outer), "or": (gx + 1, outer),
    }
    to = {"l": has_l, "r": has_r, "m": always, "o": has_o, "ol": has_ol, "or": has_or}
    come = {"l": has_r, "r": has_l, "m": always, "o": has_o, "ol": has_or, "or": has_ol}

    barrier = pltpu.get_barrier_semaphore()
    for name in dev:
        def hello(name=name):
            pl.semaphore_signal(barrier, inc=1, device_id=dev[name], device_id_type=MESH)
        when(to[name], hello)

    loads = [
        pltpu.make_async_copy(mem_hbm, mem, in_sem.at[0]),
        pltpu.make_async_copy(ana_hbm, ana, in_sem.at[1]),
        pltpu.make_async_copy(land_hbm, land, in_sem.at[2]),
    ]
    for load in loads:
        load.start()

    def rows64(start):
        return pl.ds(pl.multiple_of(start, PAD), PAD)

    inner_src, inner_dst = rows64(2 * PAD - PAD * par), rows64(3 * PAD * par)
    outer_src, outer_dst = rows64(PAD + PAD * par), rows64(3 * PAD - 3 * PAD * par)
    to_mate, to_outer = rows64(3 * PAD - 3 * PAD * par), rows64(3 * PAD * par)
    near_mate, near_outer = rows64(PAD - PAD * par), rows64(PAD * par)
    mates_near, outers_near = rows64(PAD * par), rows64(PAD - PAD * par)
    body = pl.ds(PAD, T)
    lane = lax.broadcasted_iota(jnp.int32, (T, T), 1)
    low = lane < PAD
    low2 = lax.broadcasted_iota(jnp.int32, (E, T), 1) < PAD

    count = [0]
    sent = []

    def send(name, src, dst, only=None):
        k = count[0]
        count[0] += 1
        copy = pltpu.make_async_remote_copy(
            src_ref=src, dst_ref=dst, send_sem=ss.at[k], recv_sem=rs.at[k],
            device_id=dev[name], device_id_type=MESH,
        )
        here, there = (to[name], come[name]) if only is None else (only, only)
        when(here, copy.start)
        sent.append((here, copy))
        return there, copy

    def arrived(item):
        when(item[0], item[1].wait_recv)

    def fill(cond, ref, rows=None):
        def zero():
            if rows is None:
                ref[...] = jnp.zeros(ref.shape, ref.dtype)
            else:
                ref[:, rows, :] = jnp.zeros((ref.shape[0], PAD, T), ref.dtype)
        pl.when(cond)(zero)

    loads[0].wait()
    loads[1].wait()
    for m in range(4):
        ctr[m, body] = mem[m] - ana[...]
    for p in range(2):
        even = ctr[2 * p, body]
        odd = pltpu.roll(ctr[2 * p + 1, body], PAD, 1)
        go_r[p] = jnp.where(low, odd, even)
        go_l[p] = jnp.where(low, even, odd)

    peers = sum(c.astype(jnp.int32) for c in (has_l, has_r, has_o, has_ol, has_or)) + 1
    pl.semaphore_wait(barrier, peers)

    mains = []
    for p in range(2):
        mains.append(send("l", go_l.at[p], rgt.at[p, body]))
        mains.append(send("r", go_r.at[p], lft.at[p, body]))
    to_o = send("o", ctr.at[:, outer_src], ctr.at[:, outer_dst])
    to_m = send("m", ctr.at[:, inner_src], ctr.at[:, inner_dst])
    corners = [
        send("ol", go_l.at[:, near_outer], rgt.at[:, outer_dst]),
        send("or", go_r.at[:, near_outer], lft.at[:, outer_dst]),
    ]

    no_l, no_r, no_o = jnp.logical_not(has_l), jnp.logical_not(has_r), jnp.logical_not(has_o)
    edge = to_outer
    fill(no_l, lft)
    fill(no_r, rgt)
    fill(jnp.logical_and(no_o, has_l), lft, edge)
    fill(jnp.logical_and(no_o, has_r), rgt, edge)
    fill(no_o, ctr, edge)
    fill(no_l, in_l)
    fill(no_r, in_r)
    fill(no_o, ud, near_outer)
    fill(jnp.logical_not(has_ol), k_l, near_outer)
    fill(jnp.logical_not(has_or), k_r, near_outer)
    k_l[:, near_mate, :] = jnp.zeros((2, PAD, T), F32)
    k_r[:, near_mate, :] = jnp.zeros((2, PAD, T), F32)

    def iota(shape, axis):
        return lax.broadcasted_iota(jnp.int32, shape, axis)

    for i, r in enumerate(RADII):
        vm[pl.ds(i * T, T), :] = band(iota((T, E), 0), iota((T, E), 1) - PAD, r)
        vt[i] = band(iota((E, T), 0) - PAD, iota((E, T), 1), r)
        for odd in range(2):
            hm[odd, i, pl.ds(0, T)] = band(iota((T, T), 0), iota((T, T), 1), r)
            hm[odd, i, pl.ds(T, T)] = band(side_column(iota((T, T), 0), odd), iota((T, T), 1), r)
            ht[odd, pl.ds(i * T, T), pl.ds(0, T)] = band(iota((T, T), 0), iota((T, T), 1), r)
            ht[odd, pl.ds(i * T, T), pl.ds(T, T)] = band(iota((T, T), 0), side_column(iota((T, T), 1), odd), r)

    arrived(to_m)
    arrived(to_o)
    v_own = []
    for p in range(2):
        wide = jnp.concatenate([ctr[2 * p], ctr[2 * p + 1]], axis=1)
        v_own.append(sum(dot(vm[...], part) for part in split(wide, 3)))

    forwards = []
    for p in range(2):
        arrived(mains[2 * p])
        arrived(mains[2 * p + 1])
        forwards.append(send("m", lft.at[p, inner_src], lft.at[p, inner_dst], has_l))
        forwards.append(send("m", rgt.at[p, inner_src], rgt.at[p, inner_dst], has_r))
    for item in corners + forwards:
        arrived(item)

    pooled = [[None] * 4 for _ in RADII]
    for p in range(2):
        a, b = lft[p], rgt[p]
        wide = jnp.concatenate([jnp.where(low2, b, a), jnp.where(low2, a, b)], axis=1)
        v_side = sum(dot(vm[...], part) for part in split(wide, 3))
        for odd in range(2):
            for i in range(3):
                rows, cols = slice(i * T, (i + 1) * T), slice(odd * T, (odd + 1) * T)
                both = jnp.concatenate([v_own[p][rows, cols], v_side[rows, cols]], axis=1)
                pooled[i][2 * p + odd] = sum(dot(part, hm[odd, i]) for part in split(both, 3))

    loads[2].wait()
    weight = land[...].astype(F32)
    for i, r in enumerate(RADII):
        soft = 0.01 * (2 * r + 1) ** 2
        one, two = weight * (1 / (4 * (2 * r + 1))), weight * (1 / (12 * (2 * r + 1)))
        q = pooled[i]
        spread = [None] * 4
        for j in range(4):
            for k in range(j + 1, 4):
                s = slope(q[j] - q[k], soft)
                spread[j] = s if spread[j] is None else spread[j] + s
                spread[k] = -s if spread[k] is None else spread[k] - s
        for j in range(4):
            value = one * slope(q[j], soft) - two * spread[j]
            for h, part in enumerate(split(value, 2)):
                sig[h, i, :, pl.ds(j * T, T)] = part

    second = []
    for p in range(2):
        frame = []
        tall = [
            sum(dot(vt[i], sig[h, i, :, pl.ds(2 * p * T, 2 * T)]) for h in range(2)) for i in range(3)
        ]
        for odd in range(2):
            cols = slice(odd * T, (odd + 1) * T)
            flat = jnp.concatenate([t[:, cols] for t in tall], axis=1)
            full = sum(dot(part, ht[odd]) for part in split(flat, 2))
            own2[2 * p + odd] = full[:, :T]
            frame.append(full[:, T:])
        s_r[p] = jnp.where(low2, frame[0], frame[1])
        s_l[p] = jnp.where(low2, frame[1], frame[0])
        give = [
            send("m", s_r.at[p, to_mate], q_r.at[p]),
            send("m", s_l.at[p, to_mate], q_l.at[p]),
        ]
        second.append(send("l", s_l.at[p, outer_src], in_r.at[p, near_outer]))
        second.append(send("r", s_r.at[p, outer_src], in_l.at[p, near_outer]))
        second.append(send("ol", s_l.at[p, to_outer], k_r.at[p, outers_near]))
        second.append(send("or", s_r.at[p, to_outer], k_l.at[p, outers_near]))
        both = pl.ds(2 * p, 2)
        second.append(send("m", own2.at[both, to_mate], ud.at[both, mates_near]))
        second.append(send("o", own2.at[both, to_outer], ud.at[both, outers_near]))
        for item in give:
            arrived(item)
        s_r[p, inner_src] = s_r[p, inner_src] + q_r[p]
        s_l[p, inner_src] = s_l[p, inner_src] + q_l[p]
        second.append(send("l", s_l.at[p, inner_src], in_r.at[p, near_mate]))
        second.append(send("r", s_r.at[p, inner_src], in_l.at[p, near_mate]))

    for item in second:
        arrived(item)
    for p in range(2):
        a, b = in_l[p] + k_l[p], in_r[p] + k_r[p]
        e, o = 2 * p, 2 * p + 1
        out_ref[e] = own2[e, body] + ud[e] + jnp.where(low, a, b)
        out_ref[o] = own2[o, body] + ud[o] + pltpu.roll(jnp.where(low, b, a), PAD, 1)
    for here, copy in sent:
        when(here, copy.wait_send)


def local(members, analysis, land_sea):
    vmem = pltpu.VMEM
    return pl.pallas_call(
        kernel,
        out_shape=jax.ShapeDtypeStruct((4, T, T), F32),
        in_specs=[pl.BlockSpec(memory_space=pl.ANY)] * 3,
        out_specs=pl.BlockSpec(memory_space=vmem),
        scratch_shapes=[
            vmem((4, T, T), F32), vmem((T, T), F32), vmem((T, T), jnp.int32),
            vmem((4, E, T), F32), vmem((2, E, T), F32), vmem((2, E, T), F32),
            vmem((2, T, T), F32), vmem((2, T, T), F32),
            vmem((3 * T, E), BF16), vmem((3, E, T), BF16),
            vmem((2, 3, E, T), BF16), vmem((2, 3 * T, E), BF16),
            vmem((2, 3, T, 4 * T), BF16),
            vmem((4, E, T), F32), vmem((2, E, T), F32), vmem((2, E, T), F32),
            vmem((2, PAD, T), F32), vmem((2, PAD, T), F32),
            vmem((4, T, T), F32),
            vmem((2, T, T), F32), vmem((2, T, T), F32), vmem((2, T, T), F32), vmem((2, T, T), F32),
            pltpu.SemaphoreType.DMA((3,)),
            pltpu.SemaphoreType.DMA((32,)), pltpu.SemaphoreType.DMA((32,)),
        ],
        compiler_params=pltpu.CompilerParams(
            collective_id=0, has_side_effects=True, vmem_limit_bytes=40 * 1024 * 1024
        ),
    )(*(pltpu.with_memory_space_constraint(x, pltpu.HBM) for x in (members, analysis, land_sea)))


def solution(mesh):
    return jax.shard_map(
        local,
        mesh=mesh,
        in_specs=(P(None, "gy", "gx"), P("gy", "gx"), P("gy", "gx")),
        out_specs=P(None, "gy", "gx"),
        check_vma=False,
    )
```

```python
import jax
import jax.numpy as jnp
from jax import lax
from jax.experimental import pallas as pl
from jax.experimental.pallas import tpu as pltpu
from jax.sharding import PartitionSpec as P

RADII = (64, 16, 4)
PAD = 64
T = 128
E = T + 2 * PAD
MESH = pl.DeviceIdType.MESH
F32 = jnp.float32
BF16 = jnp.bfloat16


def split(value, terms):
    parts = []
    for _ in range(terms - 1):
        head = value.astype(BF16)
        parts.append(head)
        value = value - head.astype(F32)
    parts.append(value.astype(BF16))
    return parts


def dot(a, b):
    return jnp.dot(a, b, preferred_element_type=F32)


def side_column(lane, odd):
    if odd:
        return jnp.where(lane < PAD, lane - PAD, lane + PAD)
    return jnp.where(lane < PAD, lane + T, lane - T)


def band(a, b, radius):
    return jnp.where(jnp.abs(a - b) <= radius, 1.0, 0.0).astype(BF16)


def slope(gap, soft):
    return gap * lax.rsqrt(gap * gap + soft)


NEAR = 16
FAR = PAD - NEAR
MID = T + 2 * NEAR


def kernel(
    mem_hbm, ana_hbm, land_hbm, out_ref,
    mem, ana, land, ctr, lft, rgt, go_l, go_r,
    vm, vs, vt, hm, ht, sig, base,
    own2, s_r, s_l, q_r, q_l, ud, in_l, in_r, k_l, k_r,
    in_sem, ss, rs, ok,
):
    gx, gy = lax.axis_index("gx"), lax.axis_index("gy")
    last_x, last_y = lax.axis_size("gx") - 1, lax.axis_size("gy") - 1
    par = lax.rem(gy, 2)
    mate = gy + 1 - 2 * par
    outer = gy - 1 + 2 * par
    has_l, has_r = gx > 0, gx < last_x
    has_o = jnp.logical_and(outer >= 0, outer <= last_y)
    has_ol, has_or = jnp.logical_and(has_l, has_o), jnp.logical_and(has_r, has_o)
    always = None

    def when(cond, fn):
        if cond is None:
            fn()
        else:
            pl.when(cond)(fn)

    dev = {
        "l": (gx - 1, gy), "r": (gx + 1, gy), "m": (gx, mate), "o": (gx, outer),
        "ol": (gx - 1, outer), "or": (gx + 1, outer),
    }
    to = {"l": has_l, "r": has_r, "m": always, "o": has_o, "ol": has_ol, "or": has_or}
    come = {"l": has_r, "r": has_l, "m": always, "o": has_o, "ol": has_or, "or": has_ol}

    def tell(semaphore, name, cond):
        def signal():
            pl.semaphore_signal(semaphore, inc=1, device_id=dev[name], device_id_type=MESH)
        when(cond, signal)

    barrier = pltpu.get_barrier_semaphore()
    for name in ("l", "r", "o", "m"):
        tell(barrier, name, to[name])

    loads = [
        pltpu.make_async_copy(mem_hbm, mem, in_sem.at[0]),
        pltpu.make_async_copy(ana_hbm, ana, in_sem.at[1]),
        pltpu.make_async_copy(land_hbm, land, in_sem.at[2]),
    ]
    for load in loads:
        load.start()

    def rows(start, size=PAD):
        return pl.ds(pl.multiple_of(start, NEAR), size)

    inner_src, inner_dst = rows(2 * PAD - PAD * par), rows(3 * PAD * par)
    outer_src, outer_dst = rows(PAD + PAD * par), rows(3 * PAD - 3 * PAD * par)
    to_mate, to_outer = rows(3 * PAD - 3 * PAD * par), rows(3 * PAD * par)
    outer_half, inner_half = rows(T * par, T), rows(T - T * par, T)
    near_mate, near_outer = rows(PAD - PAD * par), rows(PAD * par)
    mates_near, outers_near = rows(PAD * par), rows(PAD - PAD * par)
    edge_src, edge_dst = rows((T - NEAR) * par, NEAR), rows(3 * PAD - (2 * PAD + NEAR) * par, NEAR)
    far_src, far_dst = rows(NEAR + FAR * par, FAR), rows((3 * PAD + NEAR) * (1 - par), FAR)
    body, middle = pl.ds(PAD, T), pl.ds(PAD - NEAR, MID)

    def iota(shape, axis):
        return lax.broadcasted_iota(jnp.int32, shape, axis)

    low = iota((T, T), 1) < PAD
    low_mid = iota((MID, T), 1) < PAD
    low_all = iota((E, T), 1) < PAD

    count = [0]
    sent = []

    def send(name, src, dst, only=None):
        k = count[0]
        count[0] += 1
        copy = pltpu.make_async_remote_copy(
            src_ref=src, dst_ref=dst, send_sem=ss.at[k], recv_sem=rs.at[k],
            device_id=dev[name], device_id_type=MESH,
        )
        here, there = (to[name], come[name]) if only is None else (only, only)
        when(here, copy.start)
        sent.append((here, copy))
        return there, copy

    def arrived(item):
        when(item[0], item[1].wait_recv)

    def fill(cond, ref, part=None):
        def zero():
            if part is None:
                ref[...] = jnp.zeros(ref.shape, ref.dtype)
            else:
                ref[:, part, :] = jnp.zeros((ref.shape[0], PAD, T), ref.dtype)
        pl.when(cond)(zero)

    loads[0].wait()
    loads[1].wait()
    for m in range(4):
        ctr[m, body] = mem[m] - ana[...]
    for p in range(2):
        even = ctr[2 * p, body]
        odd = pltpu.roll(ctr[2 * p + 1, body], PAD, 1)
        go_r[p] = jnp.where(low, odd, even)
        go_l[p] = jnp.where(low, even, odd)

    peers = sum(c.astype(jnp.int32) for c in (has_l, has_r, has_o)) + 1
    pl.semaphore_wait(barrier, peers)

    tell(ok.at[1], "l", has_ol)
    tell(ok.at[0], "r", has_or)
    mains = []
    for p in range(2):
        mains.append(send("l", go_l.at[p], rgt.at[p, body]))
        mains.append(send("r", go_r.at[p], lft.at[p, body]))
    to_o = send("o", ctr.at[:, outer_src], ctr.at[:, outer_dst])
    to_m = send("m", ctr.at[:, inner_src], ctr.at[:, inner_dst])

    no_l, no_r, no_o = jnp.logical_not(has_l), jnp.logical_not(has_r), jnp.logical_not(has_o)
    fill(no_l, lft)
    fill(no_r, rgt)
    fill(jnp.logical_and(no_o, has_l), lft, to_outer)
    fill(jnp.logical_and(no_o, has_r), rgt, to_outer)
    fill(no_o, ctr, to_outer)
    fill(no_l, in_l)
    fill(no_r, in_r)
    fill(no_o, ud, near_outer)
    fill(jnp.logical_not(has_ol), k_l, near_outer)
    fill(jnp.logical_not(has_or), k_r, near_outer)
    k_l[:, near_mate, :] = jnp.zeros((2, PAD, T), F32)
    k_r[:, near_mate, :] = jnp.zeros((2, PAD, T), F32)

    for i, r in enumerate(RADII):
        vm[pl.ds(i * T, T), :] = band(iota((T, E), 0), iota((T, E), 1) - PAD, r)
        if i:
            vs[pl.ds((i - 1) * T, T), :] = band(iota((T, MID), 0), iota((T, MID), 1) - NEAR, r)

    when(has_ol, lambda: pl.semaphore_wait(ok.at[0], 1))
    when(has_or, lambda: pl.semaphore_wait(ok.at[1], 1))
    edges = [
        send("ol", go_l.at[:, edge_src], rgt.at[:, edge_dst]),
        send("or", go_r.at[:, edge_src], lft.at[:, edge_dst]),
    ]
    fars = [
        send("ol", go_l.at[:, far_src], rgt.at[:, far_dst]),
        send("or", go_r.at[:, far_src], lft.at[:, far_dst]),
    ]

    for i, r in enumerate(RADII):
        vt[i] = band(iota((E, T), 0) - PAD, iota((E, T), 1), r)
        for odd in range(2):
            hm[odd, i, pl.ds(0, T)] = band(iota((T, T), 0), iota((T, T), 1), r)
            hm[odd, i, pl.ds(T, T)] = band(side_column(iota((T, T), 0), odd), iota((T, T), 1), r)
            ht[odd, pl.ds(i * T, T), pl.ds(0, T)] = band(iota((T, T), 0), iota((T, T), 1), r)
            ht[odd, pl.ds(i * T, T), pl.ds(T, T)] = band(iota((T, T), 0), side_column(iota((T, T), 1), odd), r)

    arrived(to_m)
    arrived(to_o)
    v_own = []
    for p in range(2):
        wide = jnp.concatenate([ctr[2 * p], ctr[2 * p + 1]], axis=1)
        v_own.append(sum(dot(vm[...], part) for part in split(wide, 3)))

    forwards = []
    for p in range(2):
        arrived(mains[2 * p])
        arrived(mains[2 * p + 1])
        forwards.append(send("m", lft.at[p, inner_src], lft.at[p, inner_dst], has_l))
        forwards.append(send("m", rgt.at[p, inner_src], rgt.at[p, inner_dst], has_r))

    loads[2].wait()
    weight = land[...].astype(F32)

    def side(p, part, mask):
        a, b = lft[p, part], rgt[p, part]
        return jnp.concatenate([jnp.where(mask, b, a), jnp.where(mask, a, b)], axis=1)

    def pooled(i, p, odd, v_side):
        cols = slice(odd * T, (odd + 1) * T)
        both = jnp.concatenate([v_own[p][i * T : (i + 1) * T, cols], v_side[:, cols]], axis=1)
        return sum(dot(part, hm[odd, i]) for part in split(both, 3))

    def slopes(i, q):
        r = RADII[i]
        soft = 0.01 * (2 * r + 1) ** 2
        one, two = weight * (1 / (4 * (2 * r + 1))), weight * (1 / (12 * (2 * r + 1)))
        spread = [None] * 4
        for j in range(4):
            for k in range(j + 1, 4):
                s = slope(q[j] - q[k], soft)
                spread[j] = s if spread[j] is None else spread[j] + s
                spread[k] = -s if spread[k] is None else spread[k] - s
        for j in range(4):
            value = one * slope(q[j], soft) - two * spread[j]
            for h, part in enumerate(split(value, 2)):
                sig[h, i, :, pl.ds(j * T, T)] = part

    def tall(i, p, part):
        return sum(dot(vt[i, part], sig[h, i, :, pl.ds(2 * p * T, 2 * T)]) for h in range(2))

    for item in edges + forwards:
        arrived(item)
    small = []
    for p in range(2):
        small.append(sum(dot(vs[...], part) for part in split(side(p, middle, low_mid), 3)))
    for i in (1, 2):
        slopes(i, [pooled(i, m // 2, m % 2, small[m // 2][(i - 1) * T : i * T]) for m in range(4)])
    for p in range(2):
        both = [tall(i, p, pl.ds(0, E)) for i in (1, 2)]
        for odd in range(2):
            cols = slice(odd * T, (odd + 1) * T)
            flat = jnp.concatenate([t[:, cols] for t in both], axis=1)
            base[2 * p + odd] = sum(dot(part, ht[odd, pl.ds(T, 2 * T)]) for part in split(flat, 2))

    for item in fars:
        arrived(item)
    q = []
    for p in range(2):
        v_side = sum(dot(vm[pl.ds(0, T)], part) for part in split(side(p, pl.ds(0, E), low_all), 3))
        q += [pooled(0, p, odd, v_side) for odd in range(2)]
    slopes(0, q)

    def piece(p, half):
        high = tall(0, p, half)
        frame = []
        for odd in range(2):
            cols = slice(odd * T, (odd + 1) * T)
            full = base[2 * p + odd, half] + sum(
                dot(part, ht[odd, pl.ds(0, T)]) for part in split(high[:, cols], 2)
            )
            own2[2 * p + odd, half] = full[:, :T]
            frame.append(full[:, T:])
        s_r[p, half] = jnp.where(low, frame[0], frame[1])
        s_l[p, half] = jnp.where(low, frame[1], frame[0])

    second, give = [], []
    for p in range(2):
        piece(p, outer_half)
        both = pl.ds(2 * p, 2)
        second.append(send("ol", s_l.at[p, to_outer], k_r.at[p, outers_near]))
        second.append(send("or", s_r.at[p, to_outer], k_l.at[p, outers_near]))
        second.append(send("l", s_l.at[p, outer_src], in_r.at[p, near_outer]))
        second.append(send("r", s_r.at[p, outer_src], in_l.at[p, near_outer]))
        second.append(send("o", own2.at[both, to_outer], ud.at[both, outers_near]))
    for p in range(2):
        piece(p, inner_half)
        both = pl.ds(2 * p, 2)
        give.append(send("m", s_r.at[p, to_mate], q_r.at[p]))
        give.append(send("m", s_l.at[p, to_mate], q_l.at[p]))
        second.append(send("m", own2.at[both, to_mate], ud.at[both, mates_near]))
    for p in range(2):
        arrived(give[2 * p])
        arrived(give[2 * p + 1])
        s_r[p, inner_src] = s_r[p, inner_src] + q_r[p]
        s_l[p, inner_src] = s_l[p, inner_src] + q_l[p]
        second.append(send("l", s_l.at[p, inner_src], in_r.at[p, near_mate]))
        second.append(send("r", s_r.at[p, inner_src], in_l.at[p, near_mate]))

    for item in second:
        arrived(item)
    for p in range(2):
        a, b = in_l[p] + k_l[p], in_r[p] + k_r[p]
        e, o = 2 * p, 2 * p + 1
        out_ref[e] = own2[e, body] + ud[e] + jnp.where(low, a, b)
        out_ref[o] = own2[o, body] + ud[o] + pltpu.roll(jnp.where(low, b, a), PAD, 1)
    for here, copy in sent:
        when(here, copy.wait_send)


def local(members, analysis, land_sea):
    vmem = pltpu.VMEM
    return pl.pallas_call(
        kernel,
        out_shape=jax.ShapeDtypeStruct((4, T, T), F32),
        in_specs=[pl.BlockSpec(memory_space=pl.ANY)] * 3,
        out_specs=pl.BlockSpec(memory_space=vmem),
        scratch_shapes=[
            vmem((4, T, T), F32), vmem((T, T), F32), vmem((T, T), jnp.int32),
            vmem((4, E, T), F32), vmem((2, E, T), F32), vmem((2, E, T), F32),
            vmem((2, T, T), F32), vmem((2, T, T), F32),
            vmem((3 * T, E), BF16), vmem((2 * T, MID), BF16), vmem((3, E, T), BF16),
            vmem((2, 3, E, T), BF16), vmem((2, 3 * T, E), BF16),
            vmem((2, 3, T, 4 * T), BF16), vmem((4, E, E), F32),
            vmem((4, E, T), F32), vmem((2, E, T), F32), vmem((2, E, T), F32),
            vmem((2, PAD, T), F32), vmem((2, PAD, T), F32),
            vmem((4, T, T), F32),
            vmem((2, T, T), F32), vmem((2, T, T), F32), vmem((2, T, T), F32), vmem((2, T, T), F32),
            pltpu.SemaphoreType.DMA((3,)),
            pltpu.SemaphoreType.DMA((40,)), pltpu.SemaphoreType.DMA((40,)),
            pltpu.SemaphoreType.REGULAR((2,)),
        ],
        compiler_params=pltpu.CompilerParams(
            collective_id=0, has_side_effects=True, vmem_limit_bytes=40 * 1024 * 1024
        ),
    )(*(pltpu.with_memory_space_constraint(x, pltpu.HBM) for x in (members, analysis, land_sea)))


def solution(mesh):
    return jax.shard_map(
        local,
        mesh=mesh,
        in_specs=(P(None, "gy", "gx"), P("gy", "gx"), P("gy", "gx")),
        out_specs=P(None, "gy", "gx"),
        check_vma=False,
    )
```

```python
import jax
import jax.numpy as jnp
from jax import lax
from jax.experimental import pallas as pl
from jax.experimental.pallas import tpu as pltpu
from jax.sharding import PartitionSpec as P

RADII = (64, 16, 4)
PAD = 64
T = 128
E = T + 2 * PAD
MESH = pl.DeviceIdType.MESH
F32 = jnp.float32
BF16 = jnp.bfloat16


def split(value, terms):
    parts = []
    for _ in range(terms - 1):
        head = value.astype(BF16)
        parts.append(head)
        value = value - head.astype(F32)
    parts.append(value.astype(BF16))
    return parts


def dot(a, b):
    return jnp.dot(a, b, preferred_element_type=F32)


def side_column(lane, odd):
    if odd:
        return jnp.where(lane < PAD, lane - PAD, lane + PAD)
    return jnp.where(lane < PAD, lane + T, lane - T)


def band(a, b, radius):
    return jnp.where(jnp.abs(a - b) <= radius, 1.0, 0.0).astype(BF16)


def slope(gap, soft):
    return gap * lax.rsqrt(gap * gap + soft)


NEAR = 16
REST = E - PAD
LATE = PAD + 2 * NEAR


def kernel(
    mem_hbm, ana_hbm, land_hbm, out_ref,
    mem, ana, land, ctr, lft, rgt, go_l, go_r,
    vm, ve, vl, vt, hm, ht, sig, qs,
    own2, s_r, s_l, q_r, q_l, ud, in_l, in_r, k_l, k_r,
    in_sem, ss, rs, ok,
):
    gx, gy = lax.axis_index("gx"), lax.axis_index("gy")
    last_x, last_y = lax.axis_size("gx") - 1, lax.axis_size("gy") - 1
    par = lax.rem(gy, 2)
    mate = gy + 1 - 2 * par
    outer = gy - 1 + 2 * par
    has_l, has_r = gx > 0, gx < last_x
    has_o = jnp.logical_and(outer >= 0, outer <= last_y)
    has_ol, has_or = jnp.logical_and(has_l, has_o), jnp.logical_and(has_r, has_o)
    always = None

    def when(cond, fn):
        if cond is None:
            fn()
        else:
            pl.when(cond)(fn)

    dev = {
        "l": (gx - 1, gy), "r": (gx + 1, gy), "m": (gx, mate), "o": (gx, outer),
        "ol": (gx - 1, outer), "or": (gx + 1, outer),
    }
    to = {"l": has_l, "r": has_r, "m": always, "o": has_o, "ol": has_ol, "or": has_or}
    come = {"l": has_r, "r": has_l, "m": always, "o": has_o, "ol": has_or, "or": has_ol}

    def tell(semaphore, name, cond):
        def signal():
            pl.semaphore_signal(semaphore, inc=1, device_id=dev[name], device_id_type=MESH)
        when(cond, signal)

    barrier = pltpu.get_barrier_semaphore()
    for name in ("l", "r", "o", "m"):
        tell(barrier, name, to[name])

    loads = [
        pltpu.make_async_copy(mem_hbm, mem, in_sem.at[0]),
        pltpu.make_async_copy(ana_hbm, ana, in_sem.at[1]),
        pltpu.make_async_copy(land_hbm, land, in_sem.at[2]),
    ]
    for load in loads:
        load.start()

    def rows(start, size=PAD):
        return pl.ds(pl.multiple_of(start, NEAR), size)

    inner_src, inner_dst = rows(2 * PAD - PAD * par), rows(3 * PAD * par)
    outer_src, outer_dst = rows(PAD + PAD * par), rows(3 * PAD - 3 * PAD * par)
    to_mate, to_outer = rows(3 * PAD - 3 * PAD * par), rows(3 * PAD * par)
    outer_half, inner_half = rows(T * par, T), rows(T - T * par, T)
    near_mate, near_outer = rows(PAD - PAD * par), rows(PAD * par)
    mates_near, outers_near = rows(PAD * par), rows(PAD - PAD * par)
    rest = rows(PAD - PAD * par, REST)
    touched = (PAD * par, (T - NEAR) * par, (T - NEAR) * par)
    apart = (PAD - PAD * par, NEAR - NEAR * par, NEAR - NEAR * par)
    sizes = (PAD, NEAR, NEAR)
    begins = (0, PAD, PAD + NEAR)
    body = pl.ds(PAD, T)

    def iota(shape, axis):
        return lax.broadcasted_iota(jnp.int32, shape, axis)

    low = iota((T, T), 1) < PAD
    low_rest = iota((REST, T), 1) < PAD
    low_pad = iota((PAD, T), 1) < PAD

    count = [0]
    sent = []

    def send(name, src, dst, only=None):
        k = count[0]
        count[0] += 1
        copy = pltpu.make_async_remote_copy(
            src_ref=src, dst_ref=dst, send_sem=ss.at[k], recv_sem=rs.at[k],
            device_id=dev[name], device_id_type=MESH,
        )
        here, there = (to[name], come[name]) if only is None else (only, only)
        when(here, copy.start)
        sent.append((here, copy))
        return there, copy

    def arrived(item):
        when(item[0], item[1].wait_recv)

    def fill(cond, ref, part=None):
        def zero():
            if part is None:
                ref[...] = jnp.zeros(ref.shape, ref.dtype)
            else:
                ref[:, part, :] = jnp.zeros((ref.shape[0], PAD, T), ref.dtype)
        pl.when(cond)(zero)

    loads[0].wait()
    loads[1].wait()
    for m in range(4):
        ctr[m, body] = mem[m] - ana[...]
    for p in range(2):
        even = ctr[2 * p, body]
        odd = pltpu.roll(ctr[2 * p + 1, body], PAD, 1)
        go_r[p] = jnp.where(low, odd, even)
        go_l[p] = jnp.where(low, even, odd)

    peers = sum(c.astype(jnp.int32) for c in (has_l, has_r, has_o)) + 1
    pl.semaphore_wait(barrier, peers)

    tell(ok, "o", has_o)
    mains = []
    for p in range(2):
        mains.append(send("l", go_l.at[p], rgt.at[p, body]))
        mains.append(send("r", go_r.at[p], lft.at[p, body]))
    to_o = send("o", ctr.at[:, outer_src], ctr.at[:, outer_dst])
    to_m = send("m", ctr.at[:, inner_src], ctr.at[:, inner_dst])

    no_l, no_r, no_o = jnp.logical_not(has_l), jnp.logical_not(has_r), jnp.logical_not(has_o)
    fill(no_l, lft)
    fill(no_r, rgt)
    fill(jnp.logical_and(no_o, has_l), lft, to_outer)
    fill(jnp.logical_and(no_o, has_r), rgt, to_outer)
    fill(no_o, ctr, to_outer)
    fill(no_l, in_l)
    fill(no_r, in_r)
    fill(no_o, ud, near_outer)
    fill(jnp.logical_not(has_ol), k_l, near_outer)
    fill(jnp.logical_not(has_or), k_r, near_outer)
    k_l[:, near_mate, :] = jnp.zeros((2, PAD, T), F32)
    k_r[:, near_mate, :] = jnp.zeros((2, PAD, T), F32)

    for i, r in enumerate(RADII):
        whole = band(iota((T, E), 0), iota((T, E), 1) - PAD, r)
        most = band(iota((T, REST), 0), iota((T, REST), 1) - PAD * par, r)
        first = (PAD, T - NEAR, T - NEAR)[i] * par
        few = band(iota((sizes[i], PAD), 0) + first, iota((sizes[i], PAD), 1) - PAD + 3 * PAD * par, r)
        vm[pl.ds(i * T, T), :] = jnp.concatenate([whole] * 3, axis=1)
        ve[pl.ds(i * T, T), :] = jnp.concatenate([most] * 3, axis=1)
        vl[pl.ds(begins[i], sizes[i]), :] = jnp.concatenate([few] * 3, axis=1)

    when(has_o, lambda: pl.semaphore_wait(ok, 1))
    corners = [
        send("ol", go_l.at[:, near_outer], rgt.at[:, outer_dst]),
        send("or", go_r.at[:, near_outer], lft.at[:, outer_dst]),
    ]

    nought = jnp.zeros((T, T), BF16)
    for i, r in enumerate(RADII):
        square = band(iota((T, T), 0), iota((T, T), 1), r)
        sides = [band(side_column(iota((T, T), 0), odd), iota((T, T), 1), r) for odd in range(2)]
        back = [band(iota((T, T), 0), side_column(iota((T, T), 1), odd), r) for odd in range(2)]
        for first, blocks in ((0, [square, square]), (1, sides)):
            hm[first, i, pl.ds(0, T)] = jnp.concatenate([blocks[0], nought], axis=1)
            hm[first, i, pl.ds(T, T)] = jnp.concatenate([nought, blocks[1]], axis=1)
        vt[i] = jnp.concatenate([band(iota((E, T), 0) - PAD, iota((E, T), 1), r)] * 2, axis=1)
        for odd in range(2):
            for h in range(2):
                ht[odd, pl.ds((3 * h + i) * T, T)] = jnp.concatenate([square, back[odd]], axis=1)

    def along_rows(pair, first, i):
        size = pair.shape[0]
        out = dot(jnp.concatenate(split(pair, 3), axis=0), hm[first, i])
        return out[:size] + out[size : 2 * size] + out[2 * size :]

    arrived(to_m)
    arrived(to_o)
    for p in range(2):
        wide = jnp.concatenate([ctr[2 * p], ctr[2 * p + 1]], axis=1)
        v_own = dot(vm[...], jnp.concatenate(split(wide, 3), axis=0))
        for i in range(3):
            qs[i, p] = along_rows(v_own[i * T : (i + 1) * T], 0, i)

    forwards = []
    for p in range(2):
        arrived(mains[2 * p])
        arrived(mains[2 * p + 1])
        forwards.append(send("m", lft.at[p, inner_src], lft.at[p, inner_dst], has_l))
        forwards.append(send("m", rgt.at[p, inner_src], rgt.at[p, inner_dst], has_r))

    loads[2].wait()

    def side(p, part, mask):
        a, b = lft[p, part], rgt[p, part]
        return jnp.concatenate([jnp.where(mask, b, a), jnp.where(mask, a, b)], axis=1)

    def slopes(i, start, q):
        r, size = RADII[i], q[0].shape[0]
        q = [pair[:, odd * T : (odd + 1) * T] for pair in q for odd in range(2)]
        weight = land[rows(start, size)].astype(F32)
        soft = 0.01 * (2 * r + 1) ** 2
        one, two = weight * (1 / (4 * (2 * r + 1))), weight * (1 / (12 * (2 * r + 1)))
        spread = [None] * 4
        for j in range(4):
            for k in range(j + 1, 4):
                s = slope(q[j] - q[k], soft)
                spread[j] = s if spread[j] is None else spread[j] + s
                spread[k] = -s if spread[k] is None else spread[k] - s
        for j in range(4):
            value = one * slope(q[j], soft) - two * spread[j]
            for h, piece in enumerate(split(value, 2)):
                sig[i, rows(h * T + start, size), pl.ds(j * T, T)] = piece

    for p in range(2):
        arrived(forwards[2 * p])
        arrived(forwards[2 * p + 1])
        v_side = dot(ve[...], jnp.concatenate(split(side(p, rest, low_rest), 3), axis=0))
        for i in range(3):
            qs[i, p] = qs[i, p] + along_rows(v_side[i * T : (i + 1) * T], 1, i)
    for i in range(3):
        slopes(i, apart[i], [qs[i, p, rows(apart[i], T - sizes[i])] for p in range(2)])

    for item in corners:
        arrived(item)
    late = [[], [], []]
    for p in range(2):
        v_side = dot(vl[...], jnp.concatenate(split(side(p, to_outer, low_pad), 3), axis=0))
        for i in range(3):
            share = along_rows(v_side[begins[i] : begins[i] + sizes[i]], 1, i)
            late[i].append(qs[i, p, rows(touched[i], sizes[i])] + share)
    for i in range(3):
        slopes(i, touched[i], late[i])

    def piece(p, half):
        high = [dot(vt[i, half], sig[i, :, pl.ds(2 * p * T, 2 * T)]) for i in range(3)]
        frame = []
        for odd in range(2):
            flat = jnp.concatenate([t[:, odd * T : (odd + 1) * T] for t in high], axis=1)
            full = dot(jnp.concatenate(split(flat, 2), axis=1), ht[odd])
            own2[2 * p + odd, half] = full[:, :T]
            frame.append(full[:, T:])
        s_r[p, half] = jnp.where(low, frame[0], frame[1])
        s_l[p, half] = jnp.where(low, frame[1], frame[0])

    second, give = [], []
    for p in range(2):
        piece(p, outer_half)
        both = pl.ds(2 * p, 2)
        second.append(send("ol", s_l.at[p, to_outer], k_r.at[p, outers_near]))
        second.append(send("or", s_r.at[p, to_outer], k_l.at[p, outers_near]))
        second.append(send("l", s_l.at[p, outer_src], in_r.at[p, near_outer]))
        second.append(send("r", s_r.at[p, outer_src], in_l.at[p, near_outer]))
        second.append(send("o", own2.at[both, to_outer], ud.at[both, outers_near]))
    for p in range(2):
        piece(p, inner_half)
        both = pl.ds(2 * p, 2)
        give.append(send("m", s_r.at[p, to_mate], q_r.at[p]))
        give.append(send("m", s_l.at[p, to_mate], q_l.at[p]))
        second.append(send("m", own2.at[both, to_mate], ud.at[both, mates_near]))
    for p in range(2):
        arrived(give[2 * p])
        arrived(give[2 * p + 1])
        s_r[p, inner_src] = s_r[p, inner_src] + q_r[p]
        s_l[p, inner_src] = s_l[p, inner_src] + q_l[p]
        second.append(send("l", s_l.at[p, inner_src], in_r.at[p, near_mate]))
        second.append(send("r", s_r.at[p, inner_src], in_l.at[p, near_mate]))

    for item in second:
        arrived(item)
    for p in range(2):
        a, b = in_l[p] + k_l[p], in_r[p] + k_r[p]
        e, o = 2 * p, 2 * p + 1
        out_ref[e] = own2[e, body] + ud[e] + jnp.where(low, a, b)
        out_ref[o] = own2[o, body] + ud[o] + pltpu.roll(jnp.where(low, b, a), PAD, 1)
    for here, copy in sent:
        when(here, copy.wait_send)


def local(members, analysis, land_sea):
    vmem = pltpu.VMEM
    return pl.pallas_call(
        kernel,
        out_shape=jax.ShapeDtypeStruct((4, T, T), F32),
        in_specs=[pl.BlockSpec(memory_space=pl.ANY)] * 3,
        out_specs=pl.BlockSpec(memory_space=vmem),
        scratch_shapes=[
            vmem((4, T, T), F32), vmem((T, T), F32), vmem((T, T), jnp.int32),
            vmem((4, E, T), F32), vmem((2, E, T), F32), vmem((2, E, T), F32),
            vmem((2, T, T), F32), vmem((2, T, T), F32),
            vmem((3 * T, 3 * E), BF16), vmem((3 * T, 3 * REST), BF16), vmem((LATE, 3 * PAD), BF16),
            vmem((3, E, 2 * T), BF16), vmem((2, 3, E, 2 * T), BF16), vmem((2, 6 * T, E), BF16),
            vmem((3, 2 * T, 4 * T), BF16), vmem((3, 2, T, 2 * T), F32),
            vmem((4, E, T), F32), vmem((2, E, T), F32), vmem((2, E, T), F32),
            vmem((2, PAD, T), F32), vmem((2, PAD, T), F32),
            vmem((4, T, T), F32),
            vmem((2, T, T), F32), vmem((2, T, T), F32), vmem((2, T, T), F32), vmem((2, T, T), F32),
            pltpu.SemaphoreType.DMA((3,)),
            pltpu.SemaphoreType.DMA((40,)), pltpu.SemaphoreType.DMA((40,)),
            pltpu.SemaphoreType.REGULAR,
        ],
        compiler_params=pltpu.CompilerParams(
            collective_id=0, has_side_effects=True, vmem_limit_bytes=40 * 1024 * 1024
        ),
    )(*(pltpu.with_memory_space_constraint(x, pltpu.HBM) for x in (members, analysis, land_sea)))


def solution(mesh):
    return jax.shard_map(
        local,
        mesh=mesh,
        in_specs=(P(None, "gy", "gx"), P("gy", "gx"), P("gy", "gx")),
        out_specs=P(None, "gy", "gx"),
        check_vma=False,
    )
```

```python
import jax
import jax.numpy as jnp
from jax import lax
from jax.experimental import pallas as pl
from jax.experimental.pallas import tpu as pltpu
from jax.sharding import PartitionSpec as P

RADII = (64, 16, 4)
PAD = 64
T = 128
E = T + 2 * PAD
MESH = pl.DeviceIdType.MESH
F32 = jnp.float32
BF16 = jnp.bfloat16


def split(value, terms):
    parts = []
    for _ in range(terms - 1):
        head = value.astype(BF16)
        parts.append(head)
        value = value - head.astype(F32)
    parts.append(value.astype(BF16))
    return parts


def dot(a, b):
    return jnp.dot(a, b, preferred_element_type=F32)


def side_column(lane, odd):
    if odd:
        return jnp.where(lane < PAD, lane - PAD, lane + PAD)
    return jnp.where(lane < PAD, lane + T, lane - T)


def band(a, b, radius):
    return jnp.where(jnp.abs(a - b) <= radius, 1.0, 0.0).astype(BF16)


def slope(gap, soft):
    return gap * lax.rsqrt(gap * gap + soft)


NEAR = 16
REST = E - PAD
LATE = PAD + 2 * NEAR


def kernel(
    mem_hbm, ana_hbm, land_hbm, out_ref,
    mem, ana, land, ctr, lft, rgt, go_l, go_r,
    vm, ve, vl, vt, hm, ht, sig, qs,
    own2, s_r, s_l, q_r, q_l, ud, in_l, in_r, k_l, k_r,
    in_sem, ss, rs, ok,
):
    gx, gy = lax.axis_index("gx"), lax.axis_index("gy")
    last_x, last_y = lax.axis_size("gx") - 1, lax.axis_size("gy") - 1
    par = lax.rem(gy, 2)
    mate = gy + 1 - 2 * par
    outer = gy - 1 + 2 * par
    has_l, has_r = gx > 0, gx < last_x
    has_o = jnp.logical_and(outer >= 0, outer <= last_y)
    has_ol, has_or = jnp.logical_and(has_l, has_o), jnp.logical_and(has_r, has_o)
    always = None

    def when(cond, fn):
        if cond is None:
            fn()
        else:
            pl.when(cond)(fn)

    dev = {
        "l": (gx - 1, gy), "r": (gx + 1, gy), "m": (gx, mate), "o": (gx, outer),
        "ol": (gx - 1, outer), "or": (gx + 1, outer),
    }
    to = {"l": has_l, "r": has_r, "m": always, "o": has_o, "ol": has_ol, "or": has_or}
    come = {"l": has_r, "r": has_l, "m": always, "o": has_o, "ol": has_or, "or": has_ol}

    def tell(semaphore, name, cond):
        def signal():
            pl.semaphore_signal(semaphore, inc=1, device_id=dev[name], device_id_type=MESH)
        when(cond, signal)

    barrier = pltpu.get_barrier_semaphore()
    for name in ("l", "r", "o", "m"):
        tell(barrier, name, to[name])

    loads = [
        pltpu.make_async_copy(mem_hbm, mem, in_sem.at[0]),
        pltpu.make_async_copy(ana_hbm, ana, in_sem.at[1]),
        pltpu.make_async_copy(land_hbm, land, in_sem.at[2]),
    ]
    for load in loads:
        load.start()

    def rows(start, size=PAD):
        return pl.ds(pl.multiple_of(start, NEAR), size)

    inner_src, inner_dst = rows(2 * PAD - PAD * par), rows(3 * PAD * par)
    outer_src, outer_dst = rows(PAD + PAD * par), rows(3 * PAD - 3 * PAD * par)
    to_mate, to_outer = rows(3 * PAD - 3 * PAD * par), rows(3 * PAD * par)
    outer_half, inner_half = rows(T * par, T), rows(T - T * par, T)
    near_mate, near_outer = rows(PAD - PAD * par), rows(PAD * par)
    mates_near, outers_near = rows(PAD * par), rows(PAD - PAD * par)
    rest = rows(PAD - PAD * par, REST)
    touched = (PAD * par, (T - NEAR) * par, (T - NEAR) * par)
    apart = (PAD - PAD * par, NEAR - NEAR * par, NEAR - NEAR * par)
    sizes = (PAD, NEAR, NEAR)
    begins = (0, PAD, PAD + NEAR)
    body = pl.ds(PAD, T)

    def iota(shape, axis):
        return lax.broadcasted_iota(jnp.int32, shape, axis)

    low = iota((T, T), 1) < PAD
    low_rest = iota((REST, T), 1) < PAD
    low_pad = iota((PAD, T), 1) < PAD

    count = [0]
    sent = []

    def send(name, src, dst, only=None):
        k = count[0]
        count[0] += 1
        copy = pltpu.make_async_remote_copy(
            src_ref=src, dst_ref=dst, send_sem=ss.at[k], recv_sem=rs.at[k],
            device_id=dev[name], device_id_type=MESH,
        )
        here, there = (to[name], come[name]) if only is None else (only, only)
        when(here, copy.start)
        sent.append((here, copy))
        return there, copy

    def arrived(item):
        when(item[0], item[1].wait_recv)

    def fill(cond, ref, part=None):
        def zero():
            if part is None:
                ref[...] = jnp.zeros(ref.shape, ref.dtype)
            else:
                ref[:, part, :] = jnp.zeros((ref.shape[0], PAD, T), ref.dtype)
        pl.when(cond)(zero)

    loads[0].wait()
    loads[1].wait()
    for m in range(4):
        ctr[m, body] = mem[m] - ana[...]
    for p in range(2):
        even = ctr[2 * p, body]
        odd = pltpu.roll(ctr[2 * p + 1, body], PAD, 1)
        go_r[p] = jnp.where(low, odd, even)
        go_l[p] = jnp.where(low, even, odd)

    peers = sum(c.astype(jnp.int32) for c in (has_l, has_r, has_o)) + 1
    pl.semaphore_wait(barrier, peers)

    tell(ok, "o", has_o)
    mains = []
    for part, there in ((near_mate, inner_src), (near_outer, outer_src)):
        mains.append(send("l", go_l.at[:, part], rgt.at[:, there]))
        mains.append(send("r", go_r.at[:, part], lft.at[:, there]))
    to_o = send("o", ctr.at[:, outer_src], ctr.at[:, outer_dst])
    to_m = send("m", ctr.at[:, inner_src], ctr.at[:, inner_dst])

    no_l, no_r, no_o = jnp.logical_not(has_l), jnp.logical_not(has_r), jnp.logical_not(has_o)
    fill(no_l, lft)
    fill(no_r, rgt)
    fill(jnp.logical_and(no_o, has_l), lft, to_outer)
    fill(jnp.logical_and(no_o, has_r), rgt, to_outer)
    fill(no_o, ctr, to_outer)
    fill(no_l, in_l)
    fill(no_r, in_r)
    fill(no_o, ud, near_outer)
    fill(jnp.logical_not(has_ol), k_l, near_outer)
    fill(jnp.logical_not(has_or), k_r, near_outer)
    k_l[:, near_mate, :] = jnp.zeros((2, PAD, T), F32)
    k_r[:, near_mate, :] = jnp.zeros((2, PAD, T), F32)

    for i, r in enumerate(RADII):
        whole = band(iota((T, E), 0), iota((T, E), 1) - PAD, r)
        most = band(iota((T, REST), 0), iota((T, REST), 1) - PAD * par, r)
        first = (PAD, T - NEAR, T - NEAR)[i] * par
        few = band(iota((sizes[i], PAD), 0) + first, iota((sizes[i], PAD), 1) - PAD + 3 * PAD * par, r)
        vm[pl.ds(i * T, T), :] = jnp.concatenate([whole] * 3, axis=1)
        ve[pl.ds(i * T, T), :] = jnp.concatenate([most] * 3, axis=1)
        vl[pl.ds(begins[i], sizes[i]), :] = jnp.concatenate([few] * 3, axis=1)

    when(has_o, lambda: pl.semaphore_wait(ok, 1))
    corners = [
        send("ol", go_l.at[:, near_outer], rgt.at[:, outer_dst]),
        send("or", go_r.at[:, near_outer], lft.at[:, outer_dst]),
    ]

    nought = jnp.zeros((T, T), BF16)
    for i, r in enumerate(RADII):
        square = band(iota((T, T), 0), iota((T, T), 1), r)
        sides = [band(side_column(iota((T, T), 0), odd), iota((T, T), 1), r) for odd in range(2)]
        back = [band(iota((T, T), 0), side_column(iota((T, T), 1), odd), r) for odd in range(2)]
        for first, blocks in ((0, [square, square]), (1, sides)):
            hm[first, i, pl.ds(0, T)] = jnp.concatenate([blocks[0], nought], axis=1)
            hm[first, i, pl.ds(T, T)] = jnp.concatenate([nought, blocks[1]], axis=1)
        vt[i] = jnp.concatenate([band(iota((E, T), 0) - PAD, iota((E, T), 1), r)] * 2, axis=1)
        for odd in range(2):
            for h in range(2):
                ht[odd, pl.ds((3 * h + i) * T, T)] = jnp.concatenate([square, back[odd]], axis=1)

    def along_rows(pair, first, i):
        size = pair.shape[0]
        out = dot(jnp.concatenate(split(pair, 3), axis=0), hm[first, i])
        return out[:size] + out[size : 2 * size] + out[2 * size :]

    arrived(to_m)
    arrived(to_o)
    for p in range(2):
        wide = jnp.concatenate([ctr[2 * p], ctr[2 * p + 1]], axis=1)
        v_own = dot(vm[...], jnp.concatenate(split(wide, 3), axis=0))
        for i in range(3):
            qs[i, p] = along_rows(v_own[i * T : (i + 1) * T], 0, i)

    arrived(mains[0])
    arrived(mains[1])
    forwards = [
        send("m", lft.at[:, inner_src], lft.at[:, inner_dst], has_l),
        send("m", rgt.at[:, inner_src], rgt.at[:, inner_dst], has_r),
    ]
    loads[2].wait()

    def side(p, part, mask):
        a, b = lft[p, part], rgt[p, part]
        return jnp.concatenate([jnp.where(mask, b, a), jnp.where(mask, a, b)], axis=1)

    def slopes(i, start, q):
        r, size = RADII[i], q[0].shape[0]
        q = [pair[:, odd * T : (odd + 1) * T] for pair in q for odd in range(2)]
        weight = land[rows(start, size)].astype(F32)
        soft = 0.01 * (2 * r + 1) ** 2
        one, two = weight * (1 / (4 * (2 * r + 1))), weight * (1 / (12 * (2 * r + 1)))
        spread = [None] * 4
        for j in range(4):
            for k in range(j + 1, 4):
                s = slope(q[j] - q[k], soft)
                spread[j] = s if spread[j] is None else spread[j] + s
                spread[k] = -s if spread[k] is None else spread[k] - s
        for j in range(4):
            value = one * slope(q[j], soft) - two * spread[j]
            for h, piece in enumerate(split(value, 2)):
                sig[i, rows(h * T + start, size), pl.ds(j * T, T)] = piece

    for item in mains[2:] + forwards:
        arrived(item)
    for p in range(2):
        v_side = dot(ve[...], jnp.concatenate(split(side(p, rest, low_rest), 3), axis=0))
        for i in range(3):
            qs[i, p] = qs[i, p] + along_rows(v_side[i * T : (i + 1) * T], 1, i)
    for i in range(3):
        slopes(i, apart[i], [qs[i, p, rows(apart[i], T - sizes[i])] for p in range(2)])

    for item in corners:
        arrived(item)
    late = [[], [], []]
    for p in range(2):
        v_side = dot(vl[...], jnp.concatenate(split(side(p, to_outer, low_pad), 3), axis=0))
        for i in range(3):
            share = along_rows(v_side[begins[i] : begins[i] + sizes[i]], 1, i)
            late[i].append(qs[i, p, rows(touched[i], sizes[i])] + share)
    for i in range(3):
        slopes(i, touched[i], late[i])

    def piece(p, half):
        high = [dot(vt[i, half], sig[i, :, pl.ds(2 * p * T, 2 * T)]) for i in range(3)]
        frame = []
        for odd in range(2):
            flat = jnp.concatenate([t[:, odd * T : (odd + 1) * T] for t in high], axis=1)
            full = dot(jnp.concatenate(split(flat, 2), axis=1), ht[odd])
            own2[2 * p + odd, half] = full[:, :T]
            frame.append(full[:, T:])
        s_r[p, half] = jnp.where(low, frame[0], frame[1])
        s_l[p, half] = jnp.where(low, frame[1], frame[0])

    second, give = [], []
    for p in (0,):
        piece(p, outer_half)
        second.append(send("ol", s_l.at[p, to_outer], k_r.at[p, outers_near]))
        second.append(send("or", s_r.at[p, to_outer], k_l.at[p, outers_near]))
        second.append(send("l", s_l.at[p, outer_src], in_r.at[p, near_outer]))
        second.append(send("r", s_r.at[p, outer_src], in_l.at[p, near_outer]))
    for p in (1,):
        piece(p, outer_half)
        second.append(send("ol", s_l.at[p, to_outer], k_r.at[p, outers_near]))
        second.append(send("or", s_r.at[p, to_outer], k_l.at[p, outers_near]))
        second.append(send("l", s_l.at[p, outer_src], in_r.at[p, near_outer]))
        second.append(send("r", s_r.at[p, outer_src], in_l.at[p, near_outer]))
    for p in range(2):
        piece(p, inner_half)
    give.append(send("m", s_r.at[:, to_mate], q_r))
    give.append(send("m", s_l.at[:, to_mate], q_l))
    arrived(give[0])
    arrived(give[1])
    s_r[:, inner_src] = s_r[:, inner_src] + q_r[...]
    s_l[:, inner_src] = s_l[:, inner_src] + q_l[...]
    second.append(send("l", s_l.at[:, inner_src], in_r.at[:, near_mate]))
    second.append(send("r", s_r.at[:, inner_src], in_l.at[:, near_mate]))
    second.append(send("o", own2.at[:, to_outer], ud.at[:, outers_near]))
    second.append(send("m", own2.at[:, to_mate], ud.at[:, mates_near]))

    for item in second:
        arrived(item)
    for p in range(2):
        a, b = in_l[p] + k_l[p], in_r[p] + k_r[p]
        e, o = 2 * p, 2 * p + 1
        out_ref[e] = own2[e, body] + ud[e] + jnp.where(low, a, b)
        out_ref[o] = own2[o, body] + ud[o] + pltpu.roll(jnp.where(low, b, a), PAD, 1)
    for here, copy in sent:
        when(here, copy.wait_send)


def local(members, analysis, land_sea):
    vmem = pltpu.VMEM
    return pl.pallas_call(
        kernel,
        out_shape=jax.ShapeDtypeStruct((4, T, T), F32),
        in_specs=[pl.BlockSpec(memory_space=pl.ANY)] * 3,
        out_specs=pl.BlockSpec(memory_space=vmem),
        scratch_shapes=[
            vmem((4, T, T), F32), vmem((T, T), F32), vmem((T, T), jnp.int32),
            vmem((4, E, T), F32), vmem((2, E, T), F32), vmem((2, E, T), F32),
            vmem((2, T, T), F32), vmem((2, T, T), F32),
            vmem((3 * T, 3 * E), BF16), vmem((3 * T, 3 * REST), BF16), vmem((LATE, 3 * PAD), BF16),
            vmem((3, E, 2 * T), BF16), vmem((2, 3, E, 2 * T), BF16), vmem((2, 6 * T, E), BF16),
            vmem((3, 2 * T, 4 * T), BF16), vmem((3, 2, T, 2 * T), F32),
            vmem((4, E, T), F32), vmem((2, E, T), F32), vmem((2, E, T), F32),
            vmem((2, PAD, T), F32), vmem((2, PAD, T), F32),
            vmem((4, T, T), F32),
            vmem((2, T, T), F32), vmem((2, T, T), F32), vmem((2, T, T), F32), vmem((2, T, T), F32),
            pltpu.SemaphoreType.DMA((3,)),
            pltpu.SemaphoreType.DMA((40,)), pltpu.SemaphoreType.DMA((40,)),
            pltpu.SemaphoreType.REGULAR,
        ],
        compiler_params=pltpu.CompilerParams(
            collective_id=0, has_side_effects=True, vmem_limit_bytes=40 * 1024 * 1024
        ),
    )(*(pltpu.with_memory_space_constraint(x, pltpu.HBM) for x in (members, analysis, land_sea)))


def solution(mesh):
    return jax.shard_map(
        local,
        mesh=mesh,
        in_specs=(P(None, "gy", "gx"), P("gy", "gx"), P("gy", "gx")),
        out_specs=P(None, "gy", "gx"),
        check_vma=False,
    )
```

```python
import jax
import jax.numpy as jnp
from jax import lax
from jax.experimental import pallas as pl
from jax.experimental.pallas import tpu as pltpu
from jax.sharding import PartitionSpec as P

RADII = (64, 16, 4)
PAD = 64
T = 128
E = T + 2 * PAD
MESH = pl.DeviceIdType.MESH
F32 = jnp.float32
BF16 = jnp.bfloat16


def split(value, terms):
    parts = []
    for _ in range(terms - 1):
        head = value.astype(BF16)
        parts.append(head)
        value = value - head.astype(F32)
    parts.append(value.astype(BF16))
    return parts


def dot(a, b):
    return jnp.dot(a, b, preferred_element_type=F32)


def side_column(lane, odd):
    if odd:
        return jnp.where(lane < PAD, lane - PAD, lane + PAD)
    return jnp.where(lane < PAD, lane + T, lane - T)


def band(a, b, radius):
    return jnp.where(jnp.abs(a - b) <= radius, 1.0, 0.0).astype(BF16)


def slope(gap, soft):
    return gap * lax.rsqrt(gap * gap + soft)


NEAR = 16
REST = E - PAD
LATE = PAD + 2 * NEAR


def kernel(
    mem_hbm, ana_hbm, land_hbm, out_ref,
    mem, ana, land, ctr, lft, rgt, go_l, go_r,
    vm, ve, vl, vt, hm, ht, sig, qs,
    own2, s_r, s_l, q_r, q_l, ud, in_l, in_r, k_l, k_r,
    in_sem, ss, rs, ok,
):
    gx, gy = lax.axis_index("gx"), lax.axis_index("gy")
    last_x, last_y = lax.axis_size("gx") - 1, lax.axis_size("gy") - 1
    par = lax.rem(gy, 2)
    mate = gy + 1 - 2 * par
    outer = gy - 1 + 2 * par
    has_l, has_r = gx > 0, gx < last_x
    has_o = jnp.logical_and(outer >= 0, outer <= last_y)
    has_ol, has_or = jnp.logical_and(has_l, has_o), jnp.logical_and(has_r, has_o)
    always = None

    def when(cond, fn):
        if cond is None:
            fn()
        else:
            pl.when(cond)(fn)

    dev = {
        "l": (gx - 1, gy), "r": (gx + 1, gy), "m": (gx, mate), "o": (gx, outer),
        "ol": (gx - 1, outer), "or": (gx + 1, outer),
    }
    to = {"l": has_l, "r": has_r, "m": always, "o": has_o, "ol": has_ol, "or": has_or}
    come = {"l": has_r, "r": has_l, "m": always, "o": has_o, "ol": has_or, "or": has_ol}

    def tell(semaphore, name, cond):
        def signal():
            pl.semaphore_signal(semaphore, inc=1, device_id=dev[name], device_id_type=MESH)
        when(cond, signal)

    barrier = pltpu.get_barrier_semaphore()
    for name in ("l", "r", "o", "m"):
        tell(barrier, name, to[name])

    loads = [
        pltpu.make_async_copy(mem_hbm, mem, in_sem.at[0]),
        pltpu.make_async_copy(ana_hbm, ana, in_sem.at[1]),
        pltpu.make_async_copy(land_hbm, land, in_sem.at[2]),
    ]
    for load in loads:
        load.start()

    def rows(start, size=PAD):
        return pl.ds(pl.multiple_of(start, NEAR), size)

    inner_src, inner_dst = rows(2 * PAD - PAD * par), rows(3 * PAD * par)
    outer_src, outer_dst = rows(PAD + PAD * par), rows(3 * PAD - 3 * PAD * par)
    to_mate, to_outer = rows(3 * PAD - 3 * PAD * par), rows(3 * PAD * par)
    outer_half, inner_half = rows(T * par, T), rows(T - T * par, T)
    near_mate, near_outer = rows(PAD - PAD * par), rows(PAD * par)
    mates_near, outers_near = rows(PAD * par), rows(PAD - PAD * par)
    rest = rows(PAD - PAD * par, REST)
    touched = (PAD * par, (T - NEAR) * par, (T - NEAR) * par)
    apart = (PAD - PAD * par, NEAR - NEAR * par, NEAR - NEAR * par)
    sizes = (PAD, NEAR, NEAR)
    begins = (0, PAD, PAD + NEAR)
    body = pl.ds(PAD, T)

    def iota(shape, axis):
        return lax.broadcasted_iota(jnp.int32, shape, axis)

    low = iota((T, T), 1) < PAD
    low_rest = iota((REST, T), 1) < PAD
    low_pad = iota((PAD, T), 1) < PAD

    count = [0]
    sent = []

    def send(name, src, dst, only=None):
        k = count[0]
        count[0] += 1
        copy = pltpu.make_async_remote_copy(
            src_ref=src, dst_ref=dst, send_sem=ss.at[k], recv_sem=rs.at[k],
            device_id=dev[name], device_id_type=MESH,
        )
        here, there = (to[name], come[name]) if only is None else (only, only)
        when(here, copy.start)
        sent.append((here, copy))
        return there, copy

    def grouped(pairs):
        groups = {}
        for cond, wait in pairs:
            groups.setdefault(id(cond), (cond, []))[1].append(wait)
        for cond, waits in groups.values():
            when(cond, lambda waits=waits: [wait() for wait in waits] and None)

    def arrived(*items):
        grouped([(there, copy.wait_recv) for there, copy in items])

    def flush():
        grouped([(here, copy.wait_send) for here, copy in sent])
        sent.clear()

    def fill(cond, ref, part=None):
        def zero():
            if part is None:
                ref[...] = jnp.zeros(ref.shape, ref.dtype)
            else:
                ref[:, part, :] = jnp.zeros((ref.shape[0], PAD, T), ref.dtype)
        pl.when(cond)(zero)

    loads[0].wait()
    loads[1].wait()
    for m in range(4):
        ctr[m, body] = mem[m] - ana[...]
    for p in range(2):
        even = ctr[2 * p, body]
        odd = pltpu.roll(ctr[2 * p + 1, body], PAD, 1)
        go_r[p] = jnp.where(low, odd, even)
        go_l[p] = jnp.where(low, even, odd)

    peers = sum(c.astype(jnp.int32) for c in (has_l, has_r, has_o)) + 1
    pl.semaphore_wait(barrier, peers)

    tell(ok, "o", has_o)
    mains = []
    for part, there in ((near_mate, inner_src), (near_outer, outer_src)):
        mains.append(send("l", go_l.at[:, part], rgt.at[:, there]))
        mains.append(send("r", go_r.at[:, part], lft.at[:, there]))
    to_o = send("o", ctr.at[:, outer_src], ctr.at[:, outer_dst])
    to_m = send("m", ctr.at[:, inner_src], ctr.at[:, inner_dst])

    no_l, no_r, no_o = jnp.logical_not(has_l), jnp.logical_not(has_r), jnp.logical_not(has_o)
    fill(no_l, lft)
    fill(no_r, rgt)
    fill(jnp.logical_and(no_o, has_l), lft, to_outer)
    fill(jnp.logical_and(no_o, has_r), rgt, to_outer)
    fill(no_o, ctr, to_outer)
    fill(no_l, in_l)
    fill(no_r, in_r)
    fill(no_o, ud, near_outer)
    fill(jnp.logical_not(has_ol), k_l, near_outer)
    fill(jnp.logical_not(has_or), k_r, near_outer)
    k_l[:, near_mate, :] = jnp.zeros((2, PAD, T), F32)
    k_r[:, near_mate, :] = jnp.zeros((2, PAD, T), F32)

    for i, r in enumerate(RADII):
        whole = band(iota((T, E), 0), iota((T, E), 1) - PAD, r)
        most = band(iota((T, REST), 0), iota((T, REST), 1) - PAD * par, r)
        first = (PAD, T - NEAR, T - NEAR)[i] * par
        few = band(iota((sizes[i], PAD), 0) + first, iota((sizes[i], PAD), 1) - PAD + 3 * PAD * par, r)
        vm[pl.ds(i * T, T), :] = jnp.concatenate([whole] * 3, axis=1)
        ve[pl.ds(i * T, T), :] = jnp.concatenate([most] * 3, axis=1)
        vl[pl.ds(begins[i], sizes[i]), :] = jnp.concatenate([few] * 3, axis=1)

    when(has_o, lambda: pl.semaphore_wait(ok, 1))
    corners = [
        send("ol", go_l.at[:, near_outer], rgt.at[:, outer_dst]),
        send("or", go_r.at[:, near_outer], lft.at[:, outer_dst]),
    ]

    nought = jnp.zeros((T, T), BF16)
    for i, r in enumerate(RADII):
        square = band(iota((T, T), 0), iota((T, T), 1), r)
        sides = [band(side_column(iota((T, T), 0), odd), iota((T, T), 1), r) for odd in range(2)]
        back = [band(iota((T, T), 0), side_column(iota((T, T), 1), odd), r) for odd in range(2)]
        for first, blocks in ((0, [square, square]), (1, sides)):
            hm[first, i, pl.ds(0, T)] = jnp.concatenate([blocks[0], nought], axis=1)
            hm[first, i, pl.ds(T, T)] = jnp.concatenate([nought, blocks[1]], axis=1)
        vt[i] = jnp.concatenate([band(iota((E, T), 0) - PAD, iota((E, T), 1), r)] * 2, axis=1)
        for odd in range(2):
            for h in range(2):
                ht[odd, pl.ds((3 * h + i) * T, T)] = jnp.concatenate([square, back[odd]], axis=1)

    def along_rows(pairs, first, i):
        size = pairs[0].shape[0]
        out = dot(jnp.concatenate([term for pair in pairs for term in split(pair, 3)], axis=0), hm[first, i])
        out = [out[k * size : (k + 1) * size] for k in range(3 * len(pairs))]
        return [out[3 * k] + out[3 * k + 1] + out[3 * k + 2] for k in range(len(pairs))]

    arrived(to_m, to_o)
    v_own = []
    for p in range(2):
        wide = jnp.concatenate([ctr[2 * p], ctr[2 * p + 1]], axis=1)
        v_own.append(dot(vm[...], jnp.concatenate(split(wide, 3), axis=0)))
    for i in range(3):
        for p, out in enumerate(along_rows([v[i * T : (i + 1) * T] for v in v_own], 0, i)):
            qs[i, p] = out

    arrived(*mains[:2])
    forwards = [
        send("m", lft.at[:, inner_src], lft.at[:, inner_dst], has_l),
        send("m", rgt.at[:, inner_src], rgt.at[:, inner_dst], has_r),
    ]
    loads[2].wait()

    def side(p, part, mask):
        a, b = lft[p, part], rgt[p, part]
        return jnp.concatenate([jnp.where(mask, b, a), jnp.where(mask, a, b)], axis=1)

    def slopes(i, start, q):
        r, size = RADII[i], q[0].shape[0]
        q = [pair[:, odd * T : (odd + 1) * T] for pair in q for odd in range(2)]
        weight = land[rows(start, size)].astype(F32)
        soft = 0.01 * (2 * r + 1) ** 2
        one, two = weight * (1 / (4 * (2 * r + 1))), weight * (1 / (12 * (2 * r + 1)))
        spread = [None] * 4
        for j in range(4):
            for k in range(j + 1, 4):
                s = slope(q[j] - q[k], soft)
                spread[j] = s if spread[j] is None else spread[j] + s
                spread[k] = -s if spread[k] is None else spread[k] - s
        for j in range(4):
            value = one * slope(q[j], soft) - two * spread[j]
            for h, piece in enumerate(split(value, 2)):
                sig[i, rows(h * T + start, size), pl.ds(j * T, T)] = piece

    arrived(*mains[2:], *forwards)
    v_side = [
        dot(ve[...], jnp.concatenate(split(side(p, rest, low_rest), 3), axis=0)) for p in range(2)
    ]
    for i in range(3):
        for p, out in enumerate(along_rows([v[i * T : (i + 1) * T] for v in v_side], 1, i)):
            qs[i, p] = qs[i, p] + out
    for i in range(3):
        slopes(i, apart[i], [qs[i, p, rows(apart[i], T - sizes[i])] for p in range(2)])

    arrived(*corners)
    v_side = [
        dot(vl[...], jnp.concatenate(split(side(p, to_outer, low_pad), 3), axis=0)) for p in range(2)
    ]
    for i in range(3):
        share = along_rows([v[begins[i] : begins[i] + sizes[i]] for v in v_side], 1, i)
        slopes(i, touched[i], [qs[i, p, rows(touched[i], sizes[i])] + share[p] for p in range(2)])

    def piece(todo):
        flat = [[], []]
        for p, half in todo:
            high = [dot(vt[i, half], sig[i, :, pl.ds(2 * p * T, 2 * T)]) for i in range(3)]
            for odd in range(2):
                one = jnp.concatenate([t[:, odd * T : (odd + 1) * T] for t in high], axis=1)
                flat[odd].append(jnp.concatenate(split(one, 2), axis=1))
        full = [dot(jnp.concatenate(flat[odd], axis=0), ht[odd]) for odd in range(2)]
        for k, (p, half) in enumerate(todo):
            block = slice(k * T, (k + 1) * T)
            for odd in range(2):
                own2[2 * p + odd, half] = full[odd][block, :T]
            frame = [full[odd][block, T:] for odd in range(2)]
            s_r[p, half] = jnp.where(low, frame[0], frame[1])
            s_l[p, half] = jnp.where(low, frame[1], frame[0])

    old = [(here, copy.wait_send) for here, copy in sent]
    sent.clear()
    second, give = [], []
    todo = ([(0, outer_half)], [(1, outer_half), (0, inner_half), (1, inner_half)])
    for p in range(2):
        piece(todo[p])
        second.append(send("ol", s_l.at[p, to_outer], k_r.at[p, outers_near]))
        second.append(send("or", s_r.at[p, to_outer], k_l.at[p, outers_near]))
        second.append(send("l", s_l.at[p, outer_src], in_r.at[p, near_outer]))
        second.append(send("r", s_r.at[p, outer_src], in_l.at[p, near_outer]))
    give.append(send("m", s_r.at[:, to_mate], q_r))
    give.append(send("m", s_l.at[:, to_mate], q_l))
    arrived(*give)
    s_r[:, inner_src] = s_r[:, inner_src] + q_r[...]
    s_l[:, inner_src] = s_l[:, inner_src] + q_l[...]
    second.append(send("l", s_l.at[:, inner_src], in_r.at[:, near_mate]))
    second.append(send("r", s_r.at[:, inner_src], in_l.at[:, near_mate]))
    second.append(send("o", own2.at[:, to_outer], ud.at[:, outers_near]))
    second.append(send("m", own2.at[:, to_mate], ud.at[:, mates_near]))

    grouped(old)
    arrived(*second)
    for p in range(2):
        a, b = in_l[p] + k_l[p], in_r[p] + k_r[p]
        e, o = 2 * p, 2 * p + 1
        out_ref[e] = own2[e, body] + ud[e] + jnp.where(low, a, b)
        out_ref[o] = own2[o, body] + ud[o] + pltpu.roll(jnp.where(low, b, a), PAD, 1)
    flush()


def local(members, analysis, land_sea):
    vmem = pltpu.VMEM
    return pl.pallas_call(
        kernel,
        out_shape=jax.ShapeDtypeStruct((4, T, T), F32),
        in_specs=[pl.BlockSpec(memory_space=pl.ANY)] * 3,
        out_specs=pl.BlockSpec(memory_space=vmem),
        scratch_shapes=[
            vmem((4, T, T), F32), vmem((T, T), F32), vmem((T, T), jnp.int32),
            vmem((4, E, T), F32), vmem((2, E, T), F32), vmem((2, E, T), F32),
            vmem((2, T, T), F32), vmem((2, T, T), F32),
            vmem((3 * T, 3 * E), BF16), vmem((3 * T, 3 * REST), BF16), vmem((LATE, 3 * PAD), BF16),
            vmem((3, E, 2 * T), BF16), vmem((2, 3, E, 2 * T), BF16), vmem((2, 6 * T, E), BF16),
            vmem((3, 2 * T, 4 * T), BF16), vmem((3, 2, T, 2 * T), F32),
            vmem((4, E, T), F32), vmem((2, E, T), F32), vmem((2, E, T), F32),
            vmem((2, PAD, T), F32), vmem((2, PAD, T), F32),
            vmem((4, T, T), F32),
            vmem((2, T, T), F32), vmem((2, T, T), F32), vmem((2, T, T), F32), vmem((2, T, T), F32),
            pltpu.SemaphoreType.DMA((3,)),
            pltpu.SemaphoreType.DMA((40,)), pltpu.SemaphoreType.DMA((40,)),
            pltpu.SemaphoreType.REGULAR,
        ],
        compiler_params=pltpu.CompilerParams(
            collective_id=0, has_side_effects=True, vmem_limit_bytes=40 * 1024 * 1024
        ),
    )(*(pltpu.with_memory_space_constraint(x, pltpu.HBM) for x in (members, analysis, land_sea)))


def solution(mesh):
    return jax.shard_map(
        local,
        mesh=mesh,
        in_specs=(P(None, "gy", "gx"), P("gy", "gx"), P("gy", "gx")),
        out_specs=P(None, "gy", "gx"),
        check_vma=False,
    )
```

```python
import jax
import jax.numpy as jnp
from jax import lax
from jax.experimental import pallas as pl
from jax.experimental.pallas import tpu as pltpu
from jax.sharding import PartitionSpec as P

RADII = (64, 16, 4)
PAD = 64
T = 128
E = T + 2 * PAD
MESH = pl.DeviceIdType.MESH
F32 = jnp.float32
BF16 = jnp.bfloat16


def split(value, terms):
    parts = []
    for _ in range(terms - 1):
        head = value.astype(BF16)
        parts.append(head)
        value = value - head.astype(F32)
    parts.append(value.astype(BF16))
    return parts


def dot(a, b):
    return jnp.dot(a, b, preferred_element_type=F32)


def side_column(lane, odd):
    if odd:
        return jnp.where(lane < PAD, lane - PAD, lane + PAD)
    return jnp.where(lane < PAD, lane + T, lane - T)


def band(a, b, radius):
    return jnp.where(jnp.abs(a - b) <= radius, 1.0, 0.0).astype(BF16)


def slope(gap, soft):
    return gap * lax.rsqrt(gap * gap + soft)


NEAR = 16
REST = E - PAD
LATE = PAD + 2 * NEAR


def kernel(
    mem_hbm, ana_hbm, land_hbm, out_ref,
    mem, ana, land, ctr, lft, rgt, go_l, go_r,
    vm, ve, vl, vt, hm, ht, sig, qs,
    own2, s_r, s_l, q_r, q_l, ud, in_l, in_r, k_l, k_r,
    in_sem, ss, rs, ok,
):
    gx, gy = lax.axis_index("gx"), lax.axis_index("gy")
    last_x, last_y = lax.axis_size("gx") - 1, lax.axis_size("gy") - 1
    par = lax.rem(gy, 2)
    mate = gy + 1 - 2 * par
    outer = gy - 1 + 2 * par
    has_l, has_r = gx > 0, gx < last_x
    has_o = jnp.logical_and(outer >= 0, outer <= last_y)
    has_ol, has_or = jnp.logical_and(has_l, has_o), jnp.logical_and(has_r, has_o)
    always = None

    def when(cond, fn):
        if cond is None:
            fn()
        else:
            pl.when(cond)(fn)

    dev = {
        "l": (gx - 1, gy), "r": (gx + 1, gy), "m": (gx, mate), "o": (gx, outer),
        "ol": (gx - 1, outer), "or": (gx + 1, outer),
    }
    to = {"l": has_l, "r": has_r, "m": always, "o": has_o, "ol": has_ol, "or": has_or}
    come = {"l": has_r, "r": has_l, "m": always, "o": has_o, "ol": has_or, "or": has_ol}

    def tell(semaphore, name, cond):
        def signal():
            pl.semaphore_signal(semaphore, inc=1, device_id=dev[name], device_id_type=MESH)
        when(cond, signal)

    barrier = pltpu.get_barrier_semaphore()
    for name in ("l", "r", "o", "m"):
        tell(barrier, name, to[name])

    loads = [
        pltpu.make_async_copy(mem_hbm, mem, in_sem.at[0]),
        pltpu.make_async_copy(ana_hbm, ana, in_sem.at[1]),
        pltpu.make_async_copy(land_hbm, land, in_sem.at[2]),
    ]
    for load in loads:
        load.start()

    def rows(start, size=PAD):
        return pl.ds(pl.multiple_of(start, NEAR), size)

    inner_src, inner_dst = rows(2 * PAD - PAD * par), rows(3 * PAD * par)
    outer_src, outer_dst = rows(PAD + PAD * par), rows(3 * PAD - 3 * PAD * par)
    to_mate, to_outer = rows(3 * PAD - 3 * PAD * par), rows(3 * PAD * par)
    outer_half, inner_half = rows(T * par, T), rows(T - T * par, T)
    near_mate, near_outer = rows(PAD - PAD * par), rows(PAD * par)
    mates_near, outers_near = rows(PAD * par), rows(PAD - PAD * par)
    rest = rows(PAD - PAD * par, REST)
    touched = (PAD * par, (T - NEAR) * par, (T - NEAR) * par)
    apart = (PAD - PAD * par, NEAR - NEAR * par, NEAR - NEAR * par)
    sizes = (PAD, NEAR, NEAR)
    begins = (0, PAD, PAD + NEAR)
    body = pl.ds(PAD, T)

    def iota(shape, axis):
        return lax.broadcasted_iota(jnp.int32, shape, axis)

    low = iota((T, T), 1) < PAD
    low_rest = iota((REST, T), 1) < PAD
    low_pad = iota((PAD, T), 1) < PAD

    count = [0]
    sent = []

    def send(name, src, dst, only=None):
        k = count[0]
        count[0] += 1
        copy = pltpu.make_async_remote_copy(
            src_ref=src, dst_ref=dst, send_sem=ss.at[k], recv_sem=rs.at[k],
            device_id=dev[name], device_id_type=MESH,
        )
        here, there = (to[name], come[name]) if only is None else (only, only)
        when(here, copy.start)
        sent.append((here, copy))
        return there, copy

    def grouped(pairs):
        groups = {}
        for cond, wait in pairs:
            groups.setdefault(id(cond), (cond, []))[1].append(wait)
        for cond, waits in groups.values():
            when(cond, lambda waits=waits: [wait() for wait in waits] and None)

    def arrived(*items):
        grouped([(there, copy.wait_recv) for there, copy in items])

    def flush():
        grouped([(here, copy.wait_send) for here, copy in sent])
        sent.clear()

    def fill(cond, ref, part=None):
        def zero():
            if part is None:
                ref[...] = jnp.zeros(ref.shape, ref.dtype)
            else:
                ref[:, part, :] = jnp.zeros((ref.shape[0], PAD, T), ref.dtype)
        pl.when(cond)(zero)

    loads[0].wait()
    loads[1].wait()
    for m in range(4):
        ctr[m, body] = mem[m] - ana[...]
    for p in range(2):
        even = ctr[2 * p, body]
        odd = pltpu.roll(ctr[2 * p + 1, body], PAD, 1)
        go_r[p] = jnp.where(low, odd, even)
        go_l[p] = jnp.where(low, even, odd)

    peers = sum(c.astype(jnp.int32) for c in (has_l, has_r, has_o)) + 1
    pl.semaphore_wait(barrier, peers)

    tell(ok, "o", has_o)
    mains = []
    for part, there in ((near_mate, inner_src), (near_outer, outer_src)):
        mains.append(send("l", go_l.at[:, part], rgt.at[:, there]))
        mains.append(send("r", go_r.at[:, part], lft.at[:, there]))
    to_o = send("o", ctr.at[:, outer_src], ctr.at[:, outer_dst])
    to_m = send("m", ctr.at[:, inner_src], ctr.at[:, inner_dst])

    no_l, no_r, no_o = jnp.logical_not(has_l), jnp.logical_not(has_r), jnp.logical_not(has_o)
    fill(no_l, lft)
    fill(no_r, rgt)
    fill(jnp.logical_and(no_o, has_l), lft, to_outer)
    fill(jnp.logical_and(no_o, has_r), rgt, to_outer)
    fill(no_o, ctr, to_outer)
    fill(no_l, in_l)
    fill(no_r, in_r)
    fill(no_o, ud, near_outer)
    fill(jnp.logical_not(has_ol), k_l, near_outer)
    fill(jnp.logical_not(has_or), k_r, near_outer)
    k_l[:, near_mate, :] = jnp.zeros((2, PAD, T), F32)
    k_r[:, near_mate, :] = jnp.zeros((2, PAD, T), F32)

    for i, r in enumerate(RADII):
        whole = band(iota((T, E), 0), iota((T, E), 1) - PAD, r)
        most = band(iota((T, REST), 0), iota((T, REST), 1) - PAD * par, r)
        first = (PAD, T - NEAR, T - NEAR)[i] * par
        few = band(iota((sizes[i], PAD), 0) + first, iota((sizes[i], PAD), 1) - PAD + 3 * PAD * par, r)
        vm[pl.ds(i * T, T), :] = jnp.concatenate([whole] * 3, axis=1)
        ve[pl.ds(i * T, T), :] = jnp.concatenate([most] * 3, axis=1)
        vl[pl.ds(begins[i], sizes[i]), :] = jnp.concatenate([few] * 3, axis=1)

    when(has_o, lambda: pl.semaphore_wait(ok, 1))
    corners = [
        send("ol", go_l.at[:, near_outer], rgt.at[:, outer_dst]),
        send("or", go_r.at[:, near_outer], lft.at[:, outer_dst]),
    ]

    nought = jnp.zeros((T, T), BF16)
    for i, r in enumerate(RADII):
        square = band(iota((T, T), 0), iota((T, T), 1), r)
        sides = [band(side_column(iota((T, T), 0), odd), iota((T, T), 1), r) for odd in range(2)]
        back = [band(iota((T, T), 0), side_column(iota((T, T), 1), odd), r) for odd in range(2)]
        for first, blocks in ((0, [square, square]), (1, sides)):
            hm[first, i, pl.ds(0, T)] = jnp.concatenate([blocks[0], nought], axis=1)
            hm[first, i, pl.ds(T, T)] = jnp.concatenate([nought, blocks[1]], axis=1)
        vt[i] = jnp.concatenate([band(iota((E, T), 0) - PAD, iota((E, T), 1), r)] * 2, axis=1)
        for odd in range(2):
            for h in range(2):
                ht[odd, pl.ds((3 * h + i) * T, T)] = jnp.concatenate([square, back[odd]], axis=1)

    def along_rows(pairs, first, i):
        size = pairs[0].shape[0]
        out = dot(jnp.concatenate([term for pair in pairs for term in split(pair, 3)], axis=0), hm[first, i])
        out = [out[k * size : (k + 1) * size] for k in range(3 * len(pairs))]
        return [out[3 * k] + out[3 * k + 1] + out[3 * k + 2] for k in range(len(pairs))]

    arrived(*mains[:2])
    forwards = [
        send("m", lft.at[:, inner_src], lft.at[:, inner_dst], has_l),
        send("m", rgt.at[:, inner_src], rgt.at[:, inner_dst], has_r),
    ]

    arrived(to_m, to_o)
    v_own = []
    for p in range(2):
        wide = jnp.concatenate([ctr[2 * p], ctr[2 * p + 1]], axis=1)
        v_own.append(dot(vm[...], jnp.concatenate(split(wide, 3), axis=0)))
    for i in range(3):
        for p, out in enumerate(along_rows([v[i * T : (i + 1) * T] for v in v_own], 0, i)):
            qs[i, p] = out

    loads[2].wait()

    def side(p, part, mask):
        a, b = lft[p, part], rgt[p, part]
        return jnp.concatenate([jnp.where(mask, b, a), jnp.where(mask, a, b)], axis=1)

    def slopes(i, start, q):
        r, size = RADII[i], q[0].shape[0]
        q = [pair[:, odd * T : (odd + 1) * T] for pair in q for odd in range(2)]
        weight = land[rows(start, size)].astype(F32)
        soft = 0.01 * (2 * r + 1) ** 2
        one, two = weight * (1 / (4 * (2 * r + 1))), weight * (1 / (12 * (2 * r + 1)))
        spread = [None] * 4
        for j in range(4):
            for k in range(j + 1, 4):
                s = slope(q[j] - q[k], soft)
                spread[j] = s if spread[j] is None else spread[j] + s
                spread[k] = -s if spread[k] is None else spread[k] - s
        for j in range(4):
            value = one * slope(q[j], soft) - two * spread[j]
            for h, piece in enumerate(split(value, 2)):
                sig[i, rows(h * T + start, size), pl.ds(j * T, T)] = piece

    arrived(*mains[2:], *forwards)
    v_side = [
        dot(ve[...], jnp.concatenate(split(side(p, rest, low_rest), 3), axis=0)) for p in range(2)
    ]
    for i in range(3):
        for p, out in enumerate(along_rows([v[i * T : (i + 1) * T] for v in v_side], 1, i)):
            qs[i, p] = qs[i, p] + out
    for i in range(3):
        slopes(i, apart[i], [qs[i, p, rows(apart[i], T - sizes[i])] for p in range(2)])

    arrived(*corners)
    v_side = [
        dot(vl[...], jnp.concatenate(split(side(p, to_outer, low_pad), 3), axis=0)) for p in range(2)
    ]
    for i in range(3):
        share = along_rows([v[begins[i] : begins[i] + sizes[i]] for v in v_side], 1, i)
        slopes(i, touched[i], [qs[i, p, rows(touched[i], sizes[i])] + share[p] for p in range(2)])

    def piece(todo):
        flat = [[], []]
        for p, half in todo:
            high = [dot(vt[i, half], sig[i, :, pl.ds(2 * p * T, 2 * T)]) for i in range(3)]
            for odd in range(2):
                one = jnp.concatenate([t[:, odd * T : (odd + 1) * T] for t in high], axis=1)
                flat[odd].append(jnp.concatenate(split(one, 2), axis=1))
        full = [dot(jnp.concatenate(flat[odd], axis=0), ht[odd]) for odd in range(2)]
        for k, (p, half) in enumerate(todo):
            block = slice(k * T, (k + 1) * T)
            for odd in range(2):
                own2[2 * p + odd, half] = full[odd][block, :T]
            frame = [full[odd][block, T:] for odd in range(2)]
            s_r[p, half] = jnp.where(low, frame[0], frame[1])
            s_l[p, half] = jnp.where(low, frame[1], frame[0])

    old = [(here, copy.wait_send) for here, copy in sent]
    sent.clear()
    second, give = [], []
    todo = ([(0, outer_half)], [(1, outer_half), (0, inner_half), (1, inner_half)])
    for p in range(2):
        piece(todo[p])
        second.append(send("ol", s_l.at[p, to_outer], k_r.at[p, outers_near]))
        second.append(send("or", s_r.at[p, to_outer], k_l.at[p, outers_near]))
        second.append(send("l", s_l.at[p, outer_src], in_r.at[p, near_outer]))
        second.append(send("r", s_r.at[p, outer_src], in_l.at[p, near_outer]))
    give.append(send("m", s_r.at[:, to_mate], q_r))
    give.append(send("m", s_l.at[:, to_mate], q_l))
    arrived(*give)
    s_r[:, inner_src] = s_r[:, inner_src] + q_r[...]
    s_l[:, inner_src] = s_l[:, inner_src] + q_l[...]
    second.append(send("l", s_l.at[:, inner_src], in_r.at[:, near_mate]))
    second.append(send("r", s_r.at[:, inner_src], in_l.at[:, near_mate]))
    second.append(send("o", own2.at[:, to_outer], ud.at[:, outers_near]))
    second.append(send("m", own2.at[:, to_mate], ud.at[:, mates_near]))

    grouped(old)
    arrived(*second)
    for p in range(2):
        a, b = in_l[p] + k_l[p], in_r[p] + k_r[p]
        e, o = 2 * p, 2 * p + 1
        out_ref[e] = own2[e, body] + ud[e] + jnp.where(low, a, b)
        out_ref[o] = own2[o, body] + ud[o] + pltpu.roll(jnp.where(low, b, a), PAD, 1)
    flush()


def local(members, analysis, land_sea):
    vmem = pltpu.VMEM
    return pl.pallas_call(
        kernel,
        out_shape=jax.ShapeDtypeStruct((4, T, T), F32),
        in_specs=[pl.BlockSpec(memory_space=pl.ANY)] * 3,
        out_specs=pl.BlockSpec(memory_space=vmem),
        scratch_shapes=[
            vmem((4, T, T), F32), vmem((T, T), F32), vmem((T, T), jnp.int32),
            vmem((4, E, T), F32), vmem((2, E, T), F32), vmem((2, E, T), F32),
            vmem((2, T, T), F32), vmem((2, T, T), F32),
            vmem((3 * T, 3 * E), BF16), vmem((3 * T, 3 * REST), BF16), vmem((LATE, 3 * PAD), BF16),
            vmem((3, E, 2 * T), BF16), vmem((2, 3, E, 2 * T), BF16), vmem((2, 6 * T, E), BF16),
            vmem((3, 2 * T, 4 * T), BF16), vmem((3, 2, T, 2 * T), F32),
            vmem((4, E, T), F32), vmem((2, E, T), F32), vmem((2, E, T), F32),
            vmem((2, PAD, T), F32), vmem((2, PAD, T), F32),
            vmem((4, T, T), F32),
            vmem((2, T, T), F32), vmem((2, T, T), F32), vmem((2, T, T), F32), vmem((2, T, T), F32),
            pltpu.SemaphoreType.DMA((3,)),
            pltpu.SemaphoreType.DMA((40,)), pltpu.SemaphoreType.DMA((40,)),
            pltpu.SemaphoreType.REGULAR,
        ],
        compiler_params=pltpu.CompilerParams(
            collective_id=0, has_side_effects=True, vmem_limit_bytes=40 * 1024 * 1024
        ),
    )(*(pltpu.with_memory_space_constraint(x, pltpu.HBM) for x in (members, analysis, land_sea)))


def solution(mesh):
    return jax.shard_map(
        local,
        mesh=mesh,
        in_specs=(P(None, "gy", "gx"), P("gy", "gx"), P("gy", "gx")),
        out_specs=P(None, "gy", "gx"),
        check_vma=False,
    )
```

```python
import jax
import jax.numpy as jnp
from jax import lax
from jax.experimental import pallas as pl
from jax.experimental.pallas import tpu as pltpu
from jax.sharding import PartitionSpec as P

RADII = (64, 16, 4)
PAD = 64
T = 128
E = T + 2 * PAD
MESH = pl.DeviceIdType.MESH
F32 = jnp.float32
BF16 = jnp.bfloat16


def split(value, terms):
    parts = []
    for _ in range(terms - 1):
        head = value.astype(BF16)
        parts.append(head)
        value = value - head.astype(F32)
    parts.append(value.astype(BF16))
    return parts


def dot(a, b):
    return jnp.dot(a, b, preferred_element_type=F32)


def side_column(lane, odd):
    if odd:
        return jnp.where(lane < PAD, lane - PAD, lane + PAD)
    return jnp.where(lane < PAD, lane + T, lane - T)


def band(a, b, radius):
    return jnp.where(jnp.abs(a - b) <= radius, 1.0, 0.0).astype(BF16)


def slope(gap, soft):
    return gap * lax.rsqrt(gap * gap + soft)


NEAR = 16
REST = E - PAD
LATE = PAD + 2 * NEAR


def kernel(
    mem_hbm, ana_hbm, land_hbm, out_ref,
    mem, ana, land, ctr, lft, rgt, go_l, go_r,
    vm, ve, vl, vt, hm, ht, sig, qs,
    own2, s_r, s_l, q_r, q_l, ud, in_l, in_r, k_l, k_r,
    in_sem, ss, rs, ok,
):
    gx, gy = lax.axis_index("gx"), lax.axis_index("gy")
    last_x, last_y = lax.axis_size("gx") - 1, lax.axis_size("gy") - 1
    par = lax.rem(gy, 2)
    mate = gy + 1 - 2 * par
    outer = gy - 1 + 2 * par
    has_l, has_r = gx > 0, gx < last_x
    has_o = jnp.logical_and(outer >= 0, outer <= last_y)
    has_ol, has_or = jnp.logical_and(has_l, has_o), jnp.logical_and(has_r, has_o)
    always = None

    def when(cond, fn):
        if cond is None:
            fn()
        else:
            pl.when(cond)(fn)

    dev = {
        "l": (gx - 1, gy), "r": (gx + 1, gy), "m": (gx, mate), "o": (gx, outer),
        "ol": (gx - 1, outer), "or": (gx + 1, outer),
    }
    to = {"l": has_l, "r": has_r, "m": always, "o": has_o, "ol": has_ol, "or": has_or}
    come = {"l": has_r, "r": has_l, "m": always, "o": has_o, "ol": has_or, "or": has_ol}

    def tell(semaphore, name, cond):
        def signal():
            pl.semaphore_signal(semaphore, inc=1, device_id=dev[name], device_id_type=MESH)
        when(cond, signal)

    barrier = pltpu.get_barrier_semaphore()
    for name in ("l", "r", "o", "m"):
        tell(barrier, name, to[name])

    loads = [
        *(pltpu.make_async_copy(mem_hbm.at[m], mem.at[m], in_sem.at[m]) for m in range(4)),
        pltpu.make_async_copy(ana_hbm, ana, in_sem.at[4]),
        pltpu.make_async_copy(land_hbm, land, in_sem.at[5]),
    ]
    for load in loads:
        load.start()

    def rows(start, size=PAD):
        return pl.ds(pl.multiple_of(start, NEAR), size)

    inner_src, inner_dst = rows(2 * PAD - PAD * par), rows(3 * PAD * par)
    outer_src, outer_dst = rows(PAD + PAD * par), rows(3 * PAD - 3 * PAD * par)
    to_mate, to_outer = rows(3 * PAD - 3 * PAD * par), rows(3 * PAD * par)
    outer_half, inner_half = rows(T * par, T), rows(T - T * par, T)
    near_mate, near_outer = rows(PAD - PAD * par), rows(PAD * par)
    mates_near, outers_near = rows(PAD * par), rows(PAD - PAD * par)
    rest = rows(PAD - PAD * par, REST)
    touched = (PAD * par, (T - NEAR) * par, (T - NEAR) * par)
    apart = (PAD - PAD * par, NEAR - NEAR * par, NEAR - NEAR * par)
    sizes = (PAD, NEAR, NEAR)
    begins = (0, PAD, PAD + NEAR)
    body = pl.ds(PAD, T)

    def iota(shape, axis):
        return lax.broadcasted_iota(jnp.int32, shape, axis)

    low = iota((T, T), 1) < PAD
    low_rest = iota((REST, T), 1) < PAD
    low_pad = iota((PAD, T), 1) < PAD

    count = [0]
    sent = []

    def send(name, src, dst, only=None):
        k = count[0]
        count[0] += 1
        copy = pltpu.make_async_remote_copy(
            src_ref=src, dst_ref=dst, send_sem=ss.at[k], recv_sem=rs.at[k],
            device_id=dev[name], device_id_type=MESH,
        )
        here, there = (to[name], come[name]) if only is None else (only, only)
        when(here, copy.start)
        sent.append((here, copy))
        return there, copy

    def grouped(pairs):
        groups = {}
        for cond, wait in pairs:
            groups.setdefault(id(cond), (cond, []))[1].append(wait)
        for cond, waits in groups.values():
            when(cond, lambda waits=waits: [wait() for wait in waits] and None)

    def arrived(*items):
        grouped([(there, copy.wait_recv) for there, copy in items])

    def flush():
        grouped([(here, copy.wait_send) for here, copy in sent])
        sent.clear()

    def fill(cond, ref, part=None):
        def zero():
            if part is None:
                ref[...] = jnp.zeros(ref.shape, ref.dtype)
            else:
                ref[:, part, :] = jnp.zeros((ref.shape[0], PAD, T), ref.dtype)
        pl.when(cond)(zero)

    for load in loads[:5]:
        load.wait()
    for m in range(4):
        ctr[m, body] = mem[m] - ana[...]
    for p in range(2):
        even = ctr[2 * p, body]
        odd = pltpu.roll(ctr[2 * p + 1, body], PAD, 1)
        go_r[p] = jnp.where(low, odd, even)
        go_l[p] = jnp.where(low, even, odd)

    peers = sum(c.astype(jnp.int32) for c in (has_l, has_r, has_o)) + 1
    pl.semaphore_wait(barrier, peers)

    tell(ok, "o", has_o)
    mains = []
    for part, there in ((near_mate, inner_src), (near_outer, outer_src)):
        mains.append(send("l", go_l.at[:, part], rgt.at[:, there]))
        mains.append(send("r", go_r.at[:, part], lft.at[:, there]))
    to_o = send("o", ctr.at[:, outer_src], ctr.at[:, outer_dst])
    to_m = send("m", ctr.at[:, inner_src], ctr.at[:, inner_dst])

    no_l, no_r, no_o = jnp.logical_not(has_l), jnp.logical_not(has_r), jnp.logical_not(has_o)
    fill(no_l, lft)
    fill(no_r, rgt)
    fill(jnp.logical_and(no_o, has_l), lft, to_outer)
    fill(jnp.logical_and(no_o, has_r), rgt, to_outer)
    fill(no_o, ctr, to_outer)
    fill(no_l, in_l)
    fill(no_r, in_r)
    fill(no_o, ud, near_outer)
    fill(jnp.logical_not(has_ol), k_l, near_outer)
    fill(jnp.logical_not(has_or), k_r, near_outer)
    k_l[:, near_mate, :] = jnp.zeros((2, PAD, T), F32)
    k_r[:, near_mate, :] = jnp.zeros((2, PAD, T), F32)

    for i, r in enumerate(RADII):
        whole = band(iota((T, E), 0), iota((T, E), 1) - PAD, r)
        most = band(iota((T, REST), 0), iota((T, REST), 1) - PAD * par, r)
        first = (PAD, T - NEAR, T - NEAR)[i] * par
        few = band(iota((sizes[i], PAD), 0) + first, iota((sizes[i], PAD), 1) - PAD + 3 * PAD * par, r)
        vm[pl.ds(i * T, T), :] = jnp.concatenate([whole] * 3, axis=1)
        ve[pl.ds(i * T, T), :] = jnp.concatenate([most] * 3, axis=1)
        vl[pl.ds(begins[i], sizes[i]), :] = jnp.concatenate([few] * 3, axis=1)

    when(has_o, lambda: pl.semaphore_wait(ok, 1))
    corners = [
        send("ol", go_l.at[:, near_outer], rgt.at[:, outer_dst]),
        send("or", go_r.at[:, near_outer], lft.at[:, outer_dst]),
    ]

    nought = jnp.zeros((T, T), BF16)
    for i, r in enumerate(RADII):
        square = band(iota((T, T), 0), iota((T, T), 1), r)
        sides = [band(side_column(iota((T, T), 0), odd), iota((T, T), 1), r) for odd in range(2)]
        back = [band(iota((T, T), 0), side_column(iota((T, T), 1), odd), r) for odd in range(2)]
        for first, blocks in ((0, [square, square]), (1, sides)):
            hm[first, i, pl.ds(0, T)] = jnp.concatenate([blocks[0], nought], axis=1)
            hm[first, i, pl.ds(T, T)] = jnp.concatenate([nought, blocks[1]], axis=1)
        vt[i] = jnp.concatenate([band(iota((E, T), 0) - PAD, iota((E, T), 1), r)] * 2, axis=1)
        for odd in range(2):
            for h in range(2):
                ht[odd, pl.ds((3 * h + i) * T, T)] = jnp.concatenate([square, back[odd]], axis=1)

    def along_rows(pairs, first, i):
        size = pairs[0].shape[0]
        out = dot(jnp.concatenate([term for pair in pairs for term in split(pair, 3)], axis=0), hm[first, i])
        out = [out[k * size : (k + 1) * size] for k in range(3 * len(pairs))]
        return [out[3 * k] + out[3 * k + 1] + out[3 * k + 2] for k in range(len(pairs))]

    arrived(*mains[:2])
    forwards = [
        send("m", lft.at[:, inner_src], lft.at[:, inner_dst], has_l),
        send("m", rgt.at[:, inner_src], rgt.at[:, inner_dst], has_r),
    ]

    arrived(to_m, to_o)
    v_own = []
    for p in range(2):
        wide = jnp.concatenate([ctr[2 * p], ctr[2 * p + 1]], axis=1)
        v_own.append(dot(vm[...], jnp.concatenate(split(wide, 3), axis=0)))
    for i in range(3):
        for p, out in enumerate(along_rows([v[i * T : (i + 1) * T] for v in v_own], 0, i)):
            qs[i, p] = out

    loads[5].wait()

    def side(p, part, mask):
        a, b = lft[p, part], rgt[p, part]
        return jnp.concatenate([jnp.where(mask, b, a), jnp.where(mask, a, b)], axis=1)

    def slopes(i, start, q):
        r, size = RADII[i], q[0].shape[0]
        q = [pair[:, odd * T : (odd + 1) * T] for pair in q for odd in range(2)]
        weight = land[rows(start, size)].astype(F32)
        soft = 0.01 * (2 * r + 1) ** 2
        one, two = weight * (1 / (4 * (2 * r + 1))), weight * (1 / (12 * (2 * r + 1)))
        spread = [None] * 4
        for j in range(4):
            for k in range(j + 1, 4):
                s = slope(q[j] - q[k], soft)
                spread[j] = s if spread[j] is None else spread[j] + s
                spread[k] = -s if spread[k] is None else spread[k] - s
        for j in range(4):
            value = one * slope(q[j], soft) - two * spread[j]
            for h, piece in enumerate(split(value, 2)):
                sig[i, rows(h * T + start, size), pl.ds(j * T, T)] = piece

    arrived(*mains[2:], *forwards)
    v_side = [
        dot(ve[...], jnp.concatenate(split(side(p, rest, low_rest), 3), axis=0)) for p in range(2)
    ]
    for i in range(3):
        for p, out in enumerate(along_rows([v[i * T : (i + 1) * T] for v in v_side], 1, i)):
            qs[i, p] = qs[i, p] + out
    for i in range(3):
        slopes(i, apart[i], [qs[i, p, rows(apart[i], T - sizes[i])] for p in range(2)])

    arrived(*corners)
    v_side = [
        dot(vl[...], jnp.concatenate(split(side(p, to_outer, low_pad), 3), axis=0)) for p in range(2)
    ]
    for i in range(3):
        share = along_rows([v[begins[i] : begins[i] + sizes[i]] for v in v_side], 1, i)
        slopes(i, touched[i], [qs[i, p, rows(touched[i], sizes[i])] + share[p] for p in range(2)])

    def piece(todo):
        flat = [[], []]
        for p, half in todo:
            high = [dot(vt[i, half], sig[i, :, pl.ds(2 * p * T, 2 * T)]) for i in range(3)]
            for odd in range(2):
                one = jnp.concatenate([t[:, odd * T : (odd + 1) * T] for t in high], axis=1)
                flat[odd].append(jnp.concatenate(split(one, 2), axis=1))
        full = [dot(jnp.concatenate(flat[odd], axis=0), ht[odd]) for odd in range(2)]
        for k, (p, half) in enumerate(todo):
            block = slice(k * T, (k + 1) * T)
            for odd in range(2):
                own2[2 * p + odd, half] = full[odd][block, :T]
            frame = [full[odd][block, T:] for odd in range(2)]
            s_r[p, half] = jnp.where(low, frame[0], frame[1])
            s_l[p, half] = jnp.where(low, frame[1], frame[0])

    old = [(here, copy.wait_send) for here, copy in sent]
    sent.clear()
    second, give = [], []
    todo = ([(0, outer_half)], [(1, outer_half), (0, inner_half), (1, inner_half)])
    for p in range(2):
        piece(todo[p])
        second.append(send("ol", s_l.at[p, to_outer], k_r.at[p, outers_near]))
        second.append(send("or", s_r.at[p, to_outer], k_l.at[p, outers_near]))
        second.append(send("l", s_l.at[p, outer_src], in_r.at[p, near_outer]))
        second.append(send("r", s_r.at[p, outer_src], in_l.at[p, near_outer]))
    give.append(send("m", s_r.at[:, to_mate], q_r))
    give.append(send("m", s_l.at[:, to_mate], q_l))
    arrived(*give)
    s_r[:, inner_src] = s_r[:, inner_src] + q_r[...]
    s_l[:, inner_src] = s_l[:, inner_src] + q_l[...]
    second.append(send("l", s_l.at[:, inner_src], in_r.at[:, near_mate]))
    second.append(send("r", s_r.at[:, inner_src], in_l.at[:, near_mate]))
    second.append(send("o", own2.at[:, to_outer], ud.at[:, outers_near]))
    second.append(send("m", own2.at[:, to_mate], ud.at[:, mates_near]))

    grouped(old)
    arrived(*second)
    for p in range(2):
        a, b = in_l[p] + k_l[p], in_r[p] + k_r[p]
        e, o = 2 * p, 2 * p + 1
        out_ref[e] = own2[e, body] + ud[e] + jnp.where(low, a, b)
        out_ref[o] = own2[o, body] + ud[o] + pltpu.roll(jnp.where(low, b, a), PAD, 1)
    flush()


def local(members, analysis, land_sea):
    vmem = pltpu.VMEM
    return pl.pallas_call(
        kernel,
        out_shape=jax.ShapeDtypeStruct((4, T, T), F32),
        in_specs=[pl.BlockSpec(memory_space=pl.ANY)] * 3,
        out_specs=pl.BlockSpec(memory_space=vmem),
        scratch_shapes=[
            vmem((4, T, T), F32), vmem((T, T), F32), vmem((T, T), jnp.int32),
            vmem((4, E, T), F32), vmem((2, E, T), F32), vmem((2, E, T), F32),
            vmem((2, T, T), F32), vmem((2, T, T), F32),
            vmem((3 * T, 3 * E), BF16), vmem((3 * T, 3 * REST), BF16), vmem((LATE, 3 * PAD), BF16),
            vmem((3, E, 2 * T), BF16), vmem((2, 3, E, 2 * T), BF16), vmem((2, 6 * T, E), BF16),
            vmem((3, 2 * T, 4 * T), BF16), vmem((3, 2, T, 2 * T), F32),
            vmem((4, E, T), F32), vmem((2, E, T), F32), vmem((2, E, T), F32),
            vmem((2, PAD, T), F32), vmem((2, PAD, T), F32),
            vmem((4, T, T), F32),
            vmem((2, T, T), F32), vmem((2, T, T), F32), vmem((2, T, T), F32), vmem((2, T, T), F32),
            pltpu.SemaphoreType.DMA((6,)),
            pltpu.SemaphoreType.DMA((40,)), pltpu.SemaphoreType.DMA((40,)),
            pltpu.SemaphoreType.REGULAR,
        ],
        compiler_params=pltpu.CompilerParams(
            collective_id=0, has_side_effects=True, vmem_limit_bytes=40 * 1024 * 1024
        ),
    )(*(pltpu.with_memory_space_constraint(x, pltpu.HBM) for x in (members, analysis, land_sea)))


def solution(mesh):
    return jax.shard_map(
        local,
        mesh=mesh,
        in_specs=(P(None, "gy", "gx"), P("gy", "gx"), P("gy", "gx")),
        out_specs=P(None, "gy", "gx"),
        check_vma=False,
    )
```

```python
import jax
import jax.numpy as jnp
from jax import lax
from jax.experimental import pallas as pl
from jax.experimental.pallas import tpu as pltpu
from jax.sharding import PartitionSpec as P

RADII = (64, 16, 4)
PAD = 64
T = 128
E = T + 2 * PAD
MESH = pl.DeviceIdType.MESH
F32 = jnp.float32
BF16 = jnp.bfloat16


def split(value, terms):
    parts = []
    for _ in range(terms - 1):
        head = value.astype(BF16)
        parts.append(head)
        value = value - head.astype(F32)
    parts.append(value.astype(BF16))
    return parts


def dot(a, b):
    return jnp.dot(a, b, preferred_element_type=F32)


def side_column(lane, odd):
    if odd:
        return jnp.where(lane < PAD, lane - PAD, lane + PAD)
    return jnp.where(lane < PAD, lane + T, lane - T)


def band(a, b, radius):
    return jnp.where(jnp.abs(a - b) <= radius, 1.0, 0.0).astype(BF16)


def slope(gap, soft):
    return gap * lax.rsqrt(gap * gap + soft)


NEAR = 16
REST = E - PAD
LATE = PAD + 2 * NEAR


def kernel(
    mem_hbm, ana_hbm, land_hbm, out_ref,
    mem, ana, land, ctr, lft, rgt, go_l, go_r,
    vm, ve, vl, vt, hm, ht, sig, qs,
    own2, s_r, s_l, q_r, q_l, ud, in_l, in_r, k_l, k_r,
    in_sem, ss, rs, ok,
):
    gx, gy = lax.axis_index("gx"), lax.axis_index("gy")
    last_x, last_y = lax.axis_size("gx") - 1, lax.axis_size("gy") - 1
    par = lax.rem(gy, 2)
    mate = gy + 1 - 2 * par
    outer = gy - 1 + 2 * par
    has_l, has_r = gx > 0, gx < last_x
    has_o = jnp.logical_and(outer >= 0, outer <= last_y)
    has_ol, has_or = jnp.logical_and(has_l, has_o), jnp.logical_and(has_r, has_o)
    always = None

    def when(cond, fn):
        if cond is None:
            fn()
        else:
            pl.when(cond)(fn)

    dev = {
        "l": (gx - 1, gy), "r": (gx + 1, gy), "m": (gx, mate), "o": (gx, outer),
        "ol": (gx - 1, outer), "or": (gx + 1, outer),
    }
    to = {"l": has_l, "r": has_r, "m": always, "o": has_o, "ol": has_ol, "or": has_or}
    come = {"l": has_r, "r": has_l, "m": always, "o": has_o, "ol": has_or, "or": has_ol}

    def tell(semaphore, name, cond):
        def signal():
            pl.semaphore_signal(semaphore, inc=1, device_id=dev[name], device_id_type=MESH)
        when(cond, signal)

    loads = [
        pltpu.make_async_copy(mem_hbm, mem, in_sem.at[0]),
        pltpu.make_async_copy(ana_hbm, ana, in_sem.at[1]),
        pltpu.make_async_copy(land_hbm, land, in_sem.at[2]),
    ]
    for load in loads:
        load.start()

    barrier = pltpu.get_barrier_semaphore()
    for name in ("l", "r", "o", "m"):
        tell(barrier, name, to[name])

    def rows(start, size=PAD):
        return pl.ds(pl.multiple_of(start, NEAR), size)

    inner_src, inner_dst = rows(2 * PAD - PAD * par), rows(3 * PAD * par)
    outer_src, outer_dst = rows(PAD + PAD * par), rows(3 * PAD - 3 * PAD * par)
    to_mate, to_outer = rows(3 * PAD - 3 * PAD * par), rows(3 * PAD * par)
    outer_half, inner_half = rows(T * par, T), rows(T - T * par, T)
    near_mate, near_outer = rows(PAD - PAD * par), rows(PAD * par)
    mates_near, outers_near = rows(PAD * par), rows(PAD - PAD * par)
    rest = rows(PAD - PAD * par, REST)
    touched = (PAD * par, (T - NEAR) * par, (T - NEAR) * par)
    apart = (PAD - PAD * par, NEAR - NEAR * par, NEAR - NEAR * par)
    sizes = (PAD, NEAR, NEAR)
    begins = (0, PAD, PAD + NEAR)
    body = pl.ds(PAD, T)

    def iota(shape, axis):
        return lax.broadcasted_iota(jnp.int32, shape, axis)

    low = iota((T, T), 1) < PAD
    low_rest = iota((REST, T), 1) < PAD
    low_pad = iota((PAD, T), 1) < PAD

    count = [0]
    sent = []

    def send(name, src, dst, only=None):
        k = count[0]
        count[0] += 1
        copy = pltpu.make_async_remote_copy(
            src_ref=src, dst_ref=dst, send_sem=ss.at[k], recv_sem=rs.at[k],
            device_id=dev[name], device_id_type=MESH,
        )
        here, there = (to[name], come[name]) if only is None else (only, only)
        when(here, copy.start)
        sent.append((here, copy))
        return there, copy

    def grouped(pairs):
        groups = {}
        for cond, wait in pairs:
            groups.setdefault(id(cond), (cond, []))[1].append(wait)
        for cond, waits in groups.values():
            when(cond, lambda waits=waits: [wait() for wait in waits] and None)

    def arrived(*items):
        grouped([(there, copy.wait_recv) for there, copy in items])

    def flush():
        grouped([(here, copy.wait_send) for here, copy in sent])
        sent.clear()

    def fill(cond, ref, part=None):
        def zero():
            if part is None:
                ref[...] = jnp.zeros(ref.shape, ref.dtype)
            else:
                ref[:, part, :] = jnp.zeros((ref.shape[0], PAD, T), ref.dtype)
        pl.when(cond)(zero)

    loads[0].wait()
    loads[1].wait()
    for m in range(4):
        ctr[m, body] = mem[m] - ana[...]
    for p in range(2):
        even = ctr[2 * p, body]
        odd = pltpu.roll(ctr[2 * p + 1, body], PAD, 1)
        go_r[p] = jnp.where(low, odd, even)
        go_l[p] = jnp.where(low, even, odd)

    peers = sum(c.astype(jnp.int32) for c in (has_l, has_r, has_o)) + 1
    pl.semaphore_wait(barrier, peers)

    tell(ok, "o", has_o)
    mains = []
    for part, there in ((near_mate, inner_src), (near_outer, outer_src)):
        mains.append(send("l", go_l.at[:, part], rgt.at[:, there]))
        mains.append(send("r", go_r.at[:, part], lft.at[:, there]))
    to_o = send("o", ctr.at[:, outer_src], ctr.at[:, outer_dst])
    to_m = send("m", ctr.at[:, inner_src], ctr.at[:, inner_dst])

    no_l, no_r, no_o = jnp.logical_not(has_l), jnp.logical_not(has_r), jnp.logical_not(has_o)
    fill(no_l, lft)
    fill(no_r, rgt)
    fill(jnp.logical_and(no_o, has_l), lft, to_outer)
    fill(jnp.logical_and(no_o, has_r), rgt, to_outer)
    fill(no_o, ctr, to_outer)
    fill(no_l, in_l)
    fill(no_r, in_r)
    fill(no_o, ud, near_outer)
    fill(jnp.logical_not(has_ol), k_l, near_outer)
    fill(jnp.logical_not(has_or), k_r, near_outer)
    k_l[:, near_mate, :] = jnp.zeros((2, PAD, T), F32)
    k_r[:, near_mate, :] = jnp.zeros((2, PAD, T), F32)

    for i, r in enumerate(RADII):
        whole = band(iota((T, E), 0), iota((T, E), 1) - PAD, r)
        most = band(iota((T, REST), 0), iota((T, REST), 1) - PAD * par, r)
        first = (PAD, T - NEAR, T - NEAR)[i] * par
        few = band(iota((sizes[i], PAD), 0) + first, iota((sizes[i], PAD), 1) - PAD + 3 * PAD * par, r)
        vm[pl.ds(i * T, T), :] = jnp.concatenate([whole] * 3, axis=1)
        ve[pl.ds(i * T, T), :] = jnp.concatenate([most] * 3, axis=1)
        vl[pl.ds(begins[i], sizes[i]), :] = jnp.concatenate([few] * 3, axis=1)

    when(has_o, lambda: pl.semaphore_wait(ok, 1))
    corners = [
        send("ol", go_l.at[:, near_outer], rgt.at[:, outer_dst]),
        send("or", go_r.at[:, near_outer], lft.at[:, outer_dst]),
    ]

    nought = jnp.zeros((T, T), BF16)
    for i, r in enumerate(RADII):
        square = band(iota((T, T), 0), iota((T, T), 1), r)
        sides = [band(side_column(iota((T, T), 0), odd), iota((T, T), 1), r) for odd in range(2)]
        back = [band(iota((T, T), 0), side_column(iota((T, T), 1), odd), r) for odd in range(2)]
        for first, blocks in ((0, [square, square]), (1, sides)):
            hm[first, i, pl.ds(0, T)] = jnp.concatenate([blocks[0], nought], axis=1)
            hm[first, i, pl.ds(T, T)] = jnp.concatenate([nought, blocks[1]], axis=1)
        vt[i] = jnp.concatenate([band(iota((E, T), 0) - PAD, iota((E, T), 1), r)] * 2, axis=1)
        for odd in range(2):
            for h in range(2):
                ht[odd, pl.ds((3 * h + i) * T, T)] = jnp.concatenate([square, back[odd]], axis=1)

    def along_rows(pairs, first, i):
        size = pairs[0].shape[0]
        out = dot(jnp.concatenate([term for pair in pairs for term in split(pair, 3)], axis=0), hm[first, i])
        out = [out[k * size : (k + 1) * size] for k in range(3 * len(pairs))]
        return [out[3 * k] + out[3 * k + 1] + out[3 * k + 2] for k in range(len(pairs))]

    arrived(*mains[:2])
    forwards = [
        send("m", lft.at[:, inner_src], lft.at[:, inner_dst], has_l),
        send("m", rgt.at[:, inner_src], rgt.at[:, inner_dst], has_r),
    ]

    arrived(to_m, to_o)
    v_own = []
    for p in range(2):
        wide = jnp.concatenate([ctr[2 * p], ctr[2 * p + 1]], axis=1)
        v_own.append(dot(vm[...], jnp.concatenate(split(wide, 3), axis=0)))
    for i in range(3):
        for p, out in enumerate(along_rows([v[i * T : (i + 1) * T] for v in v_own], 0, i)):
            qs[i, p] = out

    loads[2].wait()

    def side(p, part, mask):
        a, b = lft[p, part], rgt[p, part]
        return jnp.concatenate([jnp.where(mask, b, a), jnp.where(mask, a, b)], axis=1)

    def slopes(i, start, q):
        r, size = RADII[i], q[0].shape[0]
        q = [pair[:, odd * T : (odd + 1) * T] for pair in q for odd in range(2)]
        weight = land[rows(start, size)].astype(F32)
        soft = 0.01 * (2 * r + 1) ** 2
        one, two = weight * (1 / (4 * (2 * r + 1))), weight * (1 / (12 * (2 * r + 1)))
        spread = [None] * 4
        for j in range(4):
            for k in range(j + 1, 4):
                s = slope(q[j] - q[k], soft)
                spread[j] = s if spread[j] is None else spread[j] + s
                spread[k] = -s if spread[k] is None else spread[k] - s
        for j in range(4):
            value = one * slope(q[j], soft) - two * spread[j]
            for h, piece in enumerate(split(value, 2)):
                sig[i, rows(h * T + start, size), pl.ds(j * T, T)] = piece

    arrived(*mains[2:], *forwards)
    v_side = [
        dot(ve[...], jnp.concatenate(split(side(p, rest, low_rest), 3), axis=0)) for p in range(2)
    ]
    for i in range(3):
        for p, out in enumerate(along_rows([v[i * T : (i + 1) * T] for v in v_side], 1, i)):
            qs[i, p] = qs[i, p] + out
    for i in range(3):
        slopes(i, apart[i], [qs[i, p, rows(apart[i], T - sizes[i])] for p in range(2)])

    arrived(*corners)
    v_side = [
        dot(vl[...], jnp.concatenate(split(side(p, to_outer, low_pad), 3), axis=0)) for p in range(2)
    ]
    for i in range(3):
        share = along_rows([v[begins[i] : begins[i] + sizes[i]] for v in v_side], 1, i)
        slopes(i, touched[i], [qs[i, p, rows(touched[i], sizes[i])] + share[p] for p in range(2)])

    def piece(todo):
        flat = [[], []]
        for p, half in todo:
            high = [dot(vt[i, half], sig[i, :, pl.ds(2 * p * T, 2 * T)]) for i in range(3)]
            for odd in range(2):
                one = jnp.concatenate([t[:, odd * T : (odd + 1) * T] for t in high], axis=1)
                flat[odd].append(jnp.concatenate(split(one, 2), axis=1))
        full = [dot(jnp.concatenate(flat[odd], axis=0), ht[odd]) for odd in range(2)]
        for k, (p, half) in enumerate(todo):
            block = slice(k * T, (k + 1) * T)
            for odd in range(2):
                own2[2 * p + odd, half] = full[odd][block, :T]
            frame = [full[odd][block, T:] for odd in range(2)]
            s_r[p, half] = jnp.where(low, frame[0], frame[1])
            s_l[p, half] = jnp.where(low, frame[1], frame[0])

    old = [(here, copy.wait_send) for here, copy in sent]
    sent.clear()
    second, give = [], []
    todo = ([(0, outer_half)], [(1, outer_half), (0, inner_half), (1, inner_half)])
    for p in range(2):
        piece(todo[p])
        second.append(send("ol", s_l.at[p, to_outer], k_r.at[p, outers_near]))
        second.append(send("or", s_r.at[p, to_outer], k_l.at[p, outers_near]))
        second.append(send("l", s_l.at[p, outer_src], in_r.at[p, near_outer]))
        second.append(send("r", s_r.at[p, outer_src], in_l.at[p, near_outer]))
    give.append(send("m", s_r.at[:, to_mate], q_r))
    give.append(send("m", s_l.at[:, to_mate], q_l))
    arrived(*give)
    s_r[:, inner_src] = s_r[:, inner_src] + q_r[...]
    s_l[:, inner_src] = s_l[:, inner_src] + q_l[...]
    second.append(send("l", s_l.at[:, inner_src], in_r.at[:, near_mate]))
    second.append(send("r", s_r.at[:, inner_src], in_l.at[:, near_mate]))
    second.append(send("o", own2.at[:, to_outer], ud.at[:, outers_near]))
    second.append(send("m", own2.at[:, to_mate], ud.at[:, mates_near]))

    grouped(old)
    arrived(*second)
    for p in range(2):
        a, b = in_l[p] + k_l[p], in_r[p] + k_r[p]
        e, o = 2 * p, 2 * p + 1
        out_ref[e] = own2[e, body] + ud[e] + jnp.where(low, a, b)
        out_ref[o] = own2[o, body] + ud[o] + pltpu.roll(jnp.where(low, b, a), PAD, 1)
    flush()


def local(members, analysis, land_sea):
    vmem = pltpu.VMEM
    return pl.pallas_call(
        kernel,
        out_shape=jax.ShapeDtypeStruct((4, T, T), F32),
        in_specs=[pl.BlockSpec(memory_space=pl.ANY)] * 3,
        out_specs=pl.BlockSpec(memory_space=vmem),
        scratch_shapes=[
            vmem((4, T, T), F32), vmem((T, T), F32), vmem((T, T), jnp.int32),
            vmem((4, E, T), F32), vmem((2, E, T), F32), vmem((2, E, T), F32),
            vmem((2, T, T), F32), vmem((2, T, T), F32),
            vmem((3 * T, 3 * E), BF16), vmem((3 * T, 3 * REST), BF16), vmem((LATE, 3 * PAD), BF16),
            vmem((3, E, 2 * T), BF16), vmem((2, 3, E, 2 * T), BF16), vmem((2, 6 * T, E), BF16),
            vmem((3, 2 * T, 4 * T), BF16), vmem((3, 2, T, 2 * T), F32),
            vmem((4, E, T), F32), vmem((2, E, T), F32), vmem((2, E, T), F32),
            vmem((2, PAD, T), F32), vmem((2, PAD, T), F32),
            vmem((4, T, T), F32),
            vmem((2, T, T), F32), vmem((2, T, T), F32), vmem((2, T, T), F32), vmem((2, T, T), F32),
            pltpu.SemaphoreType.DMA((3,)),
            pltpu.SemaphoreType.DMA((40,)), pltpu.SemaphoreType.DMA((40,)),
            pltpu.SemaphoreType.REGULAR,
        ],
        compiler_params=pltpu.CompilerParams(
            collective_id=0, has_side_effects=True, vmem_limit_bytes=40 * 1024 * 1024
        ),
    )(*(pltpu.with_memory_space_constraint(x, pltpu.HBM) for x in (members, analysis, land_sea)))


def solution(mesh):
    return jax.shard_map(
        local,
        mesh=mesh,
        in_specs=(P(None, "gy", "gx"), P("gy", "gx"), P("gy", "gx")),
        out_specs=P(None, "gy", "gx"),
        check_vma=False,
    )
```
